32 devices in a mesh: groups: 2 (over y), ep: 16 (over z, x, core).
Axes of the slice: x: 2, y: 2, z: 4, core: 2. Of those that a mesh axis runs over, the one named last changes fastest.
Arguments:
- new_latent: bfloat16 [16384, 576], P(('groups', 'ep')), parts along dimension 0, may hold values from -6 to 6
- latent_gain: float32 [512], replicated, may hold values from 0.1 to 1.9
- row_slot: int32 [16384], P(('groups', 'ep')), parts along dimension 0, may hold values from 0 to 131071, as said below
- old_length: int32 [64], P(('groups', 'ep')), parts along dimension 0, may hold values from 512 to 2048, as said below
- cache: bfloat16 [64, 4096, 576], P(('groups', 'ep')), parts along dimension 0, may hold values from -6 to 6
- queries: bfloat16 [64, 2, 128, 576], P(('groups', 'ep')), parts along dimension 0, may hold values from -60 to 60
- value_up: bfloat16 [128, 512, 128], P('ep'), may hold values from -0.25 to 0.25
Outputs:
- head_values: bfloat16 [64, 2, 128, 128], P('groups', None, 'ep'), parts along dimension 0
The draws below stay inside these ranges and needn't reach their ends.
There are 2 independent parts, one for each index of `groups`. The reference program is written for one: setup_inputs(seed, part) draws one part's arguments, and reference() takes and returns one part's arrays. A program takes and returns all parts, laid end to end along the dimension named above; an argument that names none is the same for every part. Nothing has to cross between parts.
Inputs may be any that keep to these rules, and one draw needn't show every extreme that they name: `row_slot`: entry i is r * 4096 + p for the request r and position p that prefill row i fills. No two rows name the same slot, p is never below old_length[r], and the rows of one device name exactly 0 or 64 slots of the requests of each owner (owner = r // 2). `old_length`: some request has exactly 2048 rows.
All inputs are finite; a program needn't handle non-finite values.
Results may differ from the reference program's by a relative error of at most 0.0059.
Values may be sent and summed in bfloat16 or wider, within the bound.
A program may use at most 64 MiB of HBM per device.

```python
import jax
import jax.numpy as jnp
from jax import lax

HEADS = 128
LAT = 512
ROPE = 64
HD = 128
REQ_DEV = 2
QROWS = 2
PF_DEV = 512
CACHE = 4096
KVW = 576
REQUESTS = 32
PF_TOK = 8192
N_EP = 16


def layout(key):
    length_key = jax.random.fold_in(key, 101)
    choose_key = jax.random.fold_in(key, 102)
    slot_key = jax.random.fold_in(key, 103)
    route_key = jax.random.fold_in(key, 104)
    order_key = jax.random.fold_in(key, 105)
    lengths = jax.random.randint(length_key, (N_EP * REQ_DEV,), CACHE // 8, CACHE // 2 + 1, dtype=jnp.int32)
    longest = jax.random.randint(choose_key, (), 0, N_EP * REQ_DEV, dtype=jnp.int32)
    lengths = lengths.at[longest].set(CACHE // 2)
    local_slots = REQ_DEV * CACHE
    capacity = 2 * PF_DEV // N_EP
    positions = jnp.arange(CACHE, dtype=jnp.int32)
    vacant = (positions[None, None, :] >= lengths.reshape(N_EP, REQ_DEV)[:, :, None]).reshape(N_EP, local_slots).astype(jnp.int32)
    shuffled = jax.vmap(lambda sub_key: jax.random.permutation(sub_key, local_slots))(jax.random.split(slot_key, N_EP)).astype(jnp.int32)
    ranking = vacant * local_slots + shuffled
    chosen = lax.top_k(ranking, N_EP * capacity)[1].astype(jnp.int32)
    owners = jax.vmap(lambda sub_key: jax.random.permutation(sub_key, N_EP))(jax.random.split(route_key, N_EP)).astype(jnp.int32)
    owners = owners[:, :N_EP // 2]
    row_index = jnp.arange(PF_DEV, dtype=jnp.int32)
    target_owner = owners[:, row_index // capacity]
    within = (row_index % capacity)[None, :]
    sources = jnp.arange(N_EP, dtype=jnp.int32)[:, None]
    local = chosen[target_owner, sources * capacity + within]
    slots = target_owner * local_slots + local
    reorder = jax.vmap(lambda sub_key: jax.random.permutation(sub_key, PF_DEV))(jax.random.split(order_key, N_EP)).astype(jnp.int32)
    slots = jnp.take_along_axis(slots, reorder, axis=1)
    return (lengths, slots.reshape(-1))


def draw_row_slot(key, part):
    shared = layout(key)
    return shared[1]


def draw_old_length(key, part):
    shared = layout(key)
    return shared[0]


def draw_queries(key, part):
    key = jax.random.fold_in(key, 11)
    standard = jax.random.normal(key, (REQUESTS, QROWS, HEADS, LAT + ROPE), jnp.float32)
    return jnp.clip(standard, -60.0, 60.0).astype(jnp.bfloat16)


def steps_of(own_key, dims, cuts, least, top_value):
    loudness = 1.0
    for position, parts in cuts:
        steps = jax.random.uniform(jax.random.fold_in(jax.random.fold_in(own_key, 6), position), (parts,), jnp.float32, least / len(cuts), top_value / len(cuts))
        loudness = loudness * jnp.repeat(jnp.exp(steps), dims[position] // parts).reshape((-1,) + (1,) * (len(dims) - 1 - position))
    return loudness


def normal_values(key, shape, width, bound, shards=(), kind=jnp.bfloat16):
    drawn = width * jax.random.normal(key, shape, jnp.float32)
    if shards:
        drawn = drawn * steps_of(key, shape, shards, -0.22, 0.18)
    return jnp.clip(drawn, -bound, bound).astype(kind)


def setup_inputs(seed: int = 0, part: int = 0) -> dict:
    splits = jax.random.split(jax.random.key(seed), 8)
    own_keys = jax.random.split(jax.random.fold_in(splits[7], part), 8)
    return {
        "new_latent": normal_values(own_keys[0], (PF_TOK, KVW), 1.0, 6.0, ((0, 16),)),
        "latent_gain": jnp.clip(1.0 + 0.18 * jax.random.normal(splits[1], (LAT,), jnp.float32), 0.1, 1.9),
        "row_slot": draw_row_slot(jax.random.fold_in(jax.random.fold_in(splits[7], part), 71), part),
        "old_length": draw_old_length(jax.random.fold_in(jax.random.fold_in(splits[7], part), 71), part),
        "cache": normal_values(own_keys[4], (REQUESTS, CACHE, KVW), 1.0, 6.0, ((0, 16),)),
        "queries": draw_queries(jax.random.fold_in(jax.random.fold_in(splits[7], part), 71), part),
        "value_up": normal_values(splits[6], (HEADS, LAT, HD), LAT ** -0.5, 0.25, ((0, 16),)),
    }


def normalize(latent_rows, gains):
    widened = latent_rows.astype(jnp.float32)
    latent_width = gains.shape[0]
    latent_part = widened[:, :latent_width]
    factor = lax.rsqrt(lax.optimization_barrier(jnp.mean(latent_part * latent_part, axis=1, keepdims=True)) + 1e-06)
    return jnp.concatenate([latent_part * factor * gains[None, :], widened[:, latent_width:]], axis=1).astype(jnp.bfloat16)

def reference(new_latent, latent_gain, row_slot, old_length, cache, queries, value_up):
    renewed = normalize(new_latent, latent_gain)
    flattened = cache.reshape(REQUESTS * CACHE, LAT + ROPE).at[row_slot].set(renewed)
    filled = flattened.reshape(REQUESTS, CACHE, LAT + ROPE)
    written = jnp.zeros((REQUESTS * CACHE,), jnp.int32).at[row_slot].set(1).reshape(REQUESTS, CACHE)
    score_scale = (HD + ROPE) ** (-0.5)
    positions = jnp.arange(CACHE, dtype=jnp.int32)

    def attend(bundle):
        cache_rows, query_block, length, written_marks = bundle
        query_rows = query_block.reshape(QROWS * HEADS, LAT + ROPE)
        scores = lax.dot_general(query_rows, cache_rows, (((1,), (1,)), ((), ())), preferred_element_type=jnp.float32) * score_scale
        usable = (positions < length) | (written_marks > 0)
        scores = jnp.where(usable[None, :], scores, -1e+30)
        highest = lax.optimization_barrier(jnp.max(scores, axis=1, keepdims=True))
        weights = jnp.exp(scores - highest)
        denominator = lax.optimization_barrier(jnp.sum(weights, axis=1, keepdims=True))
        blended = jnp.dot(weights.astype(jnp.bfloat16), cache_rows[:, :LAT], preferred_element_type=jnp.float32) / denominator
        return blended.astype(jnp.bfloat16).reshape(QROWS, HEADS, LAT)
    latent_out = lax.map(attend, (filled, queries, old_length, written))
    projected = jnp.einsum('rqhl,hld->rqhd', latent_out.astype(jnp.float32), value_up.astype(jnp.float32))
    return projected.astype(jnp.bfloat16)
```

```python
import functools

import jax
import jax.numpy as jnp
from jax import lax
from jax.experimental import pallas as pl
from jax.experimental.pallas import tpu as pltpu
from jax.sharding import PartitionSpec as P

NT = (((1,), (1,)), ((), ()))
LANES = 128
TILE = 16
MASKED = -1e30


def flip(index, bits):
    out, place = index, 1
    while place <= bits:
        if bits & place:
            out = out + place * (1 - 2 * ((index // place) % 2))
        place *= 2
    return out


def kernel(
    dims,
    latent_ref, gain_ref, slot_ref, length_ref, cache_ref, query_ref, up_ref,
    out_ref,
    renewed, send_rows, got_rows, old_rows, queries, raw_queries, up, total, highest, denom,
    latents, got_latents,
    row_send, row_recv, lat_send, lat_recv, own_sem, load_sem,
):
    n, req, cache_len, width, lat, cap, heads, qrows, scale, chunk = dims
    me = lax.axis_index("ep")
    hpd = heads // n
    rope = width - lat
    old = cache_len // 2
    rows_req = qrows * heads
    block = qrows * hpd
    order = sorted(range(1, n), key=lambda k: -(k // 4 * 4)) if n >= 4 else list(range(1, n))
    order = [k for k in order if k >= n // 2] + [k for k in order if k < n // 2]

    barrier = pltpu.get_barrier_semaphore()
    for k in range(1, n):
        pl.semaphore_signal(
            barrier, inc=1, device_id={"ep": flip(me, k)}, device_id_type=pl.DeviceIdType.MESH
        )

    loads = [pltpu.make_async_copy(query_ref, raw_queries, load_sem.at[0])]
    for r in range(req):
        loads.append(
            pltpu.make_async_copy(
                cache_ref.at[r, pl.ds(0, old)], old_rows.at[r], load_sem.at[1 + r]
            )
        )
    loads.append(pltpu.make_async_copy(up_ref, up, load_sem.at[1 + req]))
    for load in loads:
        load.start()

    wide = latent_ref[:, :lat].astype(jnp.float32)
    factor = lax.rsqrt(jnp.mean(wide * wide, axis=1, keepdims=True) + 1e-06)
    renewed[:, :lat] = (wide * factor * gain_ref[...]).astype(jnp.bfloat16)
    count = latent_ref.shape[0]
    renewed[:, lat:] = jnp.concatenate(
        [
            latent_ref[:, lat:].astype(jnp.float32),
            jnp.zeros((count, LANES - rope), jnp.float32),
        ],
        axis=1,
    ).astype(jnp.bfloat16)

    slots = slot_ref[...]
    owners = lax.div(slots, jnp.int32(req * cache_len))
    of_request = lax.div(slots - owners * (req * cache_len), jnp.int32(cache_len))
    belongs = (lax.broadcasted_iota(jnp.int32, (n, count), 0) == owners).astype(jnp.float32)
    before = (
        lax.broadcasted_iota(jnp.int32, (count, count), 0)
        < lax.broadcasted_iota(jnp.int32, (count, count), 1)
    ).astype(jnp.float32).astype(jnp.bfloat16)
    earlier = jnp.dot(belongs.astype(jnp.bfloat16), before, preferred_element_type=jnp.float32)
    rank = jnp.sum(earlier * belongs, axis=0, keepdims=True)
    target = owners * cap + rank.astype(jnp.int32)
    flags = (
        lax.broadcasted_iota(jnp.int32, (LANES, count), 0) - rope == of_request
    ).astype(jnp.float32).astype(jnp.bfloat16)

    group = 4
    part = group * cap
    lane = lax.broadcasted_iota(jnp.int32, (part, LANES), 1)
    flagged = (lane >= rope) & (lane < rope + req)

    def fill(owner_group):
        first = owner_group * part
        choose = (
            lax.broadcasted_iota(jnp.int32, (part, count), 0) + first == target
        ).astype(jnp.float32).astype(jnp.bfloat16)
        main = jnp.dot(choose, renewed[:, :lat], preferred_element_type=jnp.float32)
        tail = jnp.dot(choose, renewed[:, lat:], preferred_element_type=jnp.float32)
        mine = lax.dot_general(choose, flags, NT, preferred_element_type=jnp.float32)
        tail = jnp.where(flagged, 1.0 - mine, tail)
        send_rows[pl.ds(owner_group * group, group), :, :lat] = (
            main.astype(jnp.bfloat16).reshape(group, cap, lat)
        )
        send_rows[pl.ds(owner_group * group, group), :, lat:] = (
            tail.astype(jnp.bfloat16).reshape(group, cap, LANES)
        )

    def row_copy(step):
        peer = flip(me, order[step])
        return pltpu.make_async_remote_copy(
            src_ref=send_rows.at[peer],
            dst_ref=got_rows.at[step],
            send_sem=row_send.at[step],
            recv_sem=row_recv.at[step],
            device_id={"ep": peer},
            device_id_type=pl.DeviceIdType.MESH,
        )

    my_group = me // group
    seen = []
    for k in order + [0]:
        if k // group not in seen:
            seen.append(k // group)
    for index, bits in enumerate(seen):
        fill(flip(my_group, bits))
        if index == 0:
            pl.semaphore_wait(barrier, n - 1)
        for step, k in enumerate(order):
            if k // group == bits:
                row_copy(step).start()
    own_rows = pltpu.make_async_copy(send_rows.at[me], got_rows.at[n - 1], own_sem.at[0])
    own_rows.start()

    loads[0].wait()
    for r in range(req):
        halves, tails = [], []
        for q in range(qrows):
            halves.append(raw_queries[r, q, :, :lat].astype(jnp.float32).reshape(n, hpd, lat))
            tails.append(raw_queries[r, q, :, lat:].astype(jnp.float32).reshape(n, hpd, rope))
        main = jnp.concatenate(halves, axis=1).reshape(rows_req, lat)
        tail = jnp.concatenate(tails, axis=1).reshape(rows_req, rope)
        extra = lax.broadcasted_iota(jnp.int32, (rows_req, LANES - rope), 1)
        tail = jnp.concatenate([tail, jnp.where(extra == r, MASKED, 0.0)], axis=1)
        queries[pl.ds(r * rows_req, rows_req), :lat] = main.astype(jnp.bfloat16)
        queries[pl.ds(r * rows_req, rows_req), lat:] = tail.astype(jnp.bfloat16)

    def absorb(where, scores, values, fresh):
        top = jnp.max(scores, axis=1, keepdims=True)
        if not fresh:
            was = highest[where, :1]
            top = jnp.maximum(top, was)
            keep = jnp.exp(was - top)
        weights = jnp.exp(scores - top)
        mass = jnp.sum(weights, axis=1, keepdims=True)
        blend = jnp.dot(weights.astype(jnp.bfloat16), values, preferred_element_type=jnp.float32)
        if not fresh:
            mass = mass + denom[where, :1] * keep
            blend = blend + total[where, :] * keep
        highest[where, :] = jnp.broadcast_to(top, (top.shape[0], LANES))
        denom[where, :] = jnp.broadcast_to(mass, (top.shape[0], LANES))
        total[where, :] = blend

    for r in range(req):
        loads[1 + r].wait()
        where = pl.ds(r * rows_req, rows_req)
        limit = length_ref[r]

        def early(i, fresh):
            keys = old_rows[r, pl.ds(i * chunk, chunk), :]
            scores = scale * lax.dot_general(
                queries[where, :width], keys, NT, preferred_element_type=jnp.float32
            )
            position = i * chunk + lax.broadcasted_iota(jnp.int32, (rows_req, chunk), 1)
            scores = jnp.where(position < limit, scores, MASKED)
            absorb(where, scores, keys[:, :lat], fresh)

        early(0, True)

        @pl.loop(1, old // chunk)
        def _(i):
            early(i, False)

    own_rows.wait()
    groups = [list(range(n - 1))[i : i + group] for i in range(0, n - 1, group)]
    for steps in groups:
        for step in steps:
            row_copy(step).wait_recv()
        first = steps[0]
        keys = got_rows[pl.ds(first, group)].reshape(part, lat + LANES)
        for r in range(req):
            where = pl.ds(r * rows_req, rows_req)
            scores = scale * lax.dot_general(
                queries[where, :], keys, NT, preferred_element_type=jnp.float32
            )
            absorb(where, scores, keys[:, :lat], False)

    for r in range(req):
        where = pl.ds(r * rows_req, rows_req)
        latents[r] = (
            (total[where, :] / denom[where, :1]).astype(jnp.bfloat16).reshape(n, block, lat)
        )

    def latent_copy(step):
        peer = flip(me, order[step])
        return pltpu.make_async_remote_copy(
            src_ref=latents.at[:, peer],
            dst_ref=got_latents.at[step],
            send_sem=lat_send.at[step],
            recv_sem=lat_recv.at[step],
            device_id={"ep": peer},
            device_id_type=pl.DeviceIdType.MESH,
        )

    for step in range(n - 1):
        latent_copy(step).start()
    own_latents = pltpu.make_async_copy(latents.at[:, me], got_latents.at[n - 1], own_sem.at[1])
    own_latents.start()

    loads[1 + req].wait()
    for step in range(n - 1):
        row_copy(step).wait_send()
    own_latents.wait()
    rows = req * block
    head_of = lax.broadcasted_iota(jnp.int32, (group * rows, out_ref.shape[1]), 0) % hpd
    for steps in groups:
        for step in steps:
            latent_copy(step).wait_recv()
        left = got_latents[pl.ds(steps[0], group)].reshape(group * rows, lat)
        result = jnp.zeros(head_of.shape, jnp.float32)
        for h in range(hpd):
            value = jnp.dot(left, up[h], preferred_element_type=jnp.float32)
            result = jnp.where(head_of == h, value, result)
        result = result.astype(jnp.bfloat16)
        for i in range(group):
            step = steps[0] + i
            source = me if step == n - 1 else flip(me, order[step])
            out_ref[pl.ds(source * rows, rows), :] = result[i * rows : (i + 1) * rows]
    for step in range(n - 1):
        latent_copy(step).wait_send()


def fused(new_latent, latent_gain, row_slot, old_length, cache, queries, value_up):
    n = lax.axis_size("ep")
    req, cache_len, width = cache.shape
    lat = latent_gain.shape[0]
    count = new_latent.shape[0]
    cap = 2 * count // n
    qrows, heads = queries.shape[1:3]
    hpd, _, hd = value_up.shape
    scale = (hd + width - lat) ** (-0.5)
    old = cache_len // 2
    rows_req = qrows * heads
    block = qrows * hpd
    dims = (n, req, cache_len, width, lat, cap, heads, qrows, scale, min(512, old))
    bf16, f32 = jnp.bfloat16, jnp.float32
    vmem = pl.BlockSpec(memory_space=pltpu.VMEM)
    hbm = pl.BlockSpec(memory_space=pl.ANY)
    smem = pl.BlockSpec(memory_space=pltpu.SMEM)
    wide = lat + LANES
    out = pl.pallas_call(
        functools.partial(kernel, dims),
        out_shape=jax.ShapeDtypeStruct((n * req * block, hd), bf16),
        in_specs=[vmem, vmem, vmem, smem, hbm, hbm, hbm],
        out_specs=vmem,
        scratch_shapes=[
            pltpu.VMEM((count, wide), bf16),
            pltpu.VMEM((n, cap, wide), bf16),
            pltpu.VMEM((n, cap, wide), bf16),
            pltpu.VMEM((req, old, width), bf16),
            pltpu.VMEM((req * rows_req, wide), bf16),
            pltpu.VMEM(queries.shape, bf16),
            pltpu.VMEM(value_up.shape, bf16),
            pltpu.VMEM((req * rows_req, lat), f32),
            pltpu.VMEM((req * rows_req, LANES), f32),
            pltpu.VMEM((req * rows_req, LANES), f32),
            pltpu.VMEM((req, n, block, lat), bf16),
            pltpu.VMEM((n, req, block, lat), bf16),
            pltpu.SemaphoreType.DMA((n,)),
            pltpu.SemaphoreType.DMA((n,)),
            pltpu.SemaphoreType.DMA((n,)),
            pltpu.SemaphoreType.DMA((n,)),
            pltpu.SemaphoreType.DMA((2,)),
            pltpu.SemaphoreType.DMA((req + 2,)),
        ],
        compiler_params=pltpu.CompilerParams(
            collective_id=0, has_side_effects=True, vmem_limit_bytes=48 * 1024 * 1024
        ),
        cost_estimate=pl.CostEstimate(
            flops=2 * req * rows_req * (old + n * cap) * (width + lat),
            bytes_accessed=2 * req * old * width,
            transcendentals=req * rows_req * (old + n * cap),
        ),
    )(new_latent, latent_gain[None, :], row_slot[None, :], old_length, cache, queries, value_up)
    return out.reshape(n * req, qrows, hpd, hd)


def normalize(latent_rows, gains):
    widened = latent_rows.astype(jnp.float32)
    latent_width = gains.shape[0]
    latent_part = widened[:, :latent_width]
    factor = lax.rsqrt(jnp.mean(latent_part * latent_part, axis=1, keepdims=True) + 1e-06)
    return jnp.concatenate(
        [latent_part * factor * gains[None, :], widened[:, latent_width:]], axis=1
    ).astype(jnp.bfloat16)


def masked_scores(query_rows, key_rows, usable, score_scale):
    scores = (
        lax.dot_general(
            query_rows, key_rows, (((1,), (1,)), ((), ())), preferred_element_type=jnp.float32
        )
        * score_scale
    )
    return jnp.where(usable[None, :], scores, -1e30)


def collective(new_latent, latent_gain, row_slot, old_length, cache, queries, value_up):
    device_count = lax.axis_size("ep")
    req_count, cache_len, row_width = cache.shape
    latent_width = latent_gain.shape[0]
    row_count = new_latent.shape[0]
    capacity = 2 * row_count // device_count
    local_slots = req_count * cache_len
    query_count = queries.shape[1]
    head_count = queries.shape[2]
    score_scale = (value_up.shape[2] + row_width - latent_width) ** (-0.5)
    renewed = normalize(new_latent, latent_gain)
    owners = row_slot // local_slots
    belongs = (owners[:, None] == jnp.arange(device_count, dtype=jnp.int32)[None, :]).astype(
        jnp.int32
    )
    earlier = jnp.cumsum(belongs, axis=0) - belongs
    order_rank = jnp.sum(earlier * belongs, axis=1)
    target = owners * capacity + order_rank
    send_rows = (
        jnp.zeros((device_count * capacity, row_width), jnp.bfloat16).at[target].set(renewed)
    )
    send_rows = send_rows.reshape(device_count, capacity, row_width)
    send_slots = (
        jnp.full((device_count * capacity,), -1, jnp.int32)
        .at[target]
        .set(row_slot - owners * local_slots)
    )
    send_slots = send_slots.reshape(device_count, capacity)
    positions = jnp.arange(cache_len, dtype=jnp.int32)
    got_rows, got_slots = (
        lax.all_to_all(send_rows, "ep", split_axis=0, concat_axis=0, tiled=True),
        lax.all_to_all(send_slots, "ep", split_axis=0, concat_axis=0, tiled=True),
    )
    got_rows = got_rows.reshape(device_count * capacity, row_width)
    got_slots = got_slots.reshape(device_count * capacity)
    outputs = []
    old_len = cache_len // 2
    for request in range(req_count):
        query_rows = queries[request].reshape(query_count * head_count, row_width)
        old_rows = cache[request, :old_len]
        early_scores = masked_scores(
            query_rows, old_rows, positions[:old_len] < old_length[request], score_scale
        )
        owned = (got_slots >= 0) & (got_slots // cache_len == request)
        late_scores = masked_scores(query_rows, got_rows, owned, score_scale)
        highest = jnp.maximum(
            jnp.max(early_scores, axis=1, keepdims=True),
            jnp.max(late_scores, axis=1, keepdims=True),
        )
        early_weights = jnp.exp(early_scores - highest)
        late_weights = jnp.exp(late_scores - highest)
        denominator = jnp.sum(early_weights, axis=1, keepdims=True) + jnp.sum(
            late_weights, axis=1, keepdims=True
        )
        blended = jnp.dot(
            early_weights.astype(jnp.bfloat16), old_rows, preferred_element_type=jnp.float32
        )
        blended = blended + jnp.dot(
            late_weights.astype(jnp.bfloat16), got_rows, preferred_element_type=jnp.float32
        )
        blended = blended[:, :latent_width] / denominator
        outputs.append(blended.astype(jnp.bfloat16).reshape(query_count, head_count, latent_width))
    latent_out = jnp.stack(outputs, axis=0)
    return jnp.einsum(
        "rqhl,hld->rqhd",
        lax.all_to_all(latent_out, "ep", split_axis=2, concat_axis=0, tiled=True),
        value_up,
        preferred_element_type=jnp.float32,
    ).astype(jnp.bfloat16)


def local(*args):
    new_latent, latent_gain, _, _, cache, queries, value_up = args
    n = lax.axis_size("ep")
    lat = latent_gain.shape[0]
    rope = cache.shape[2] - lat
    whole_tiles = (
        n % 4 == 0
        and n & (n - 1) == 0
        and (2 * new_latent.shape[0] // n) % TILE == 0
        and (queries.shape[1] * value_up.shape[0]) % TILE == 0
        and value_up.shape[0] % 8 == 0
        and lat % LANES == 0
        and rope + cache.shape[0] <= LANES
    )
    return fused(*args) if whole_tiles else collective(*args)


def solution(mesh):
    in_specs = (
        P(("groups", "ep"), None),
        P(),
        P(("groups", "ep")),
        P(("groups", "ep")),
        P(("groups", "ep"), None, None),
        P(("groups", "ep"), None, None, None),
        P("ep", None, None),
    )
    out_specs = P("groups", None, "ep", None)
    return jax.shard_map(local, mesh=mesh, in_specs=in_specs, out_specs=out_specs, check_vma=False)
```

```python
import functools

import jax
import jax.numpy as jnp
from jax import lax
from jax.experimental import pallas as pl
from jax.experimental.pallas import tpu as pltpu
from jax.sharding import PartitionSpec as P

NN = (((1,), (0,)), ((), ()))
NT = (((1,), (1,)), ((), ()))
LANES = 128
TILE = 16
MASKED = -1e30


def flip(index, bits):
    out, place = index, 1
    while place <= bits:
        if bits & place:
            out = out + place * (1 - 2 * ((index // place) % 2))
        place *= 2
    return out


def kernel(
    dims,
    latent_ref, gain_ref, slot_ref, length_ref, cache_ref, query_ref, up_ref,
    out_ref,
    renewed, send_rows, got_rows, old_rows, queries, raw_queries, up, total, highest, denom,
    latents, got_latents,
    row_send, row_recv, lat_send, lat_recv, own_sem, load_sem,
):
    n, req, cache_len, width, lat, cap, heads, qrows, scale, chunk = dims
    me = lax.axis_index("ep")
    hpd = heads // n
    rope = width - lat
    old = cache_len // 2
    rows_req = qrows * heads
    block = qrows * hpd
    order = sorted(range(1, n), key=lambda k: -(k // 4 * 4)) if n >= 4 else list(range(1, n))
    order = [k for k in order if k >= n // 2] + [k for k in order if k < n // 2]

    barrier = pltpu.get_barrier_semaphore()
    for k in range(1, n):
        pl.semaphore_signal(
            barrier, inc=1, device_id={"ep": flip(me, k)}, device_id_type=pl.DeviceIdType.MESH
        )

    loads = [pltpu.make_async_copy(query_ref, raw_queries, load_sem.at[0])]
    for r in range(req):
        loads.append(
            pltpu.make_async_copy(
                cache_ref.at[r, :, pl.ds(0, old)], old_rows.at[r], load_sem.at[1 + r]
            )
        )
    loads.append(pltpu.make_async_copy(up_ref, up, load_sem.at[1 + req]))
    for load in loads:
        load.start()

    count = latent_ref.shape[1]
    wide = latent_ref[:lat, :].astype(jnp.float32)
    factor = lax.rsqrt(jnp.mean(wide * wide, axis=0, keepdims=True) + 1e-06)
    gains = jnp.transpose(jnp.broadcast_to(gain_ref[...], (LANES, lat)))
    gains = jnp.concatenate([gains] * (count // LANES), axis=1)
    renewed[:lat, :] = (wide * factor * gains).astype(jnp.bfloat16)
    renewed[lat:width, :] = latent_ref[lat:, :]
    renewed[width:, :] = jnp.zeros((lat + LANES - width, count), jnp.bfloat16)

    slots = slot_ref[...]
    owners = lax.div(slots, jnp.int32(req * cache_len))
    of_request = lax.div(slots - owners * (req * cache_len), jnp.int32(cache_len))
    belongs = (lax.broadcasted_iota(jnp.int32, (n, count), 0) == owners).astype(jnp.float32)
    before = (
        lax.broadcasted_iota(jnp.int32, (count, count), 0)
        < lax.broadcasted_iota(jnp.int32, (count, count), 1)
    ).astype(jnp.float32).astype(jnp.bfloat16)
    earlier = jnp.dot(belongs.astype(jnp.bfloat16), before, preferred_element_type=jnp.float32)
    rank = jnp.sum(earlier * belongs, axis=0, keepdims=True)
    target = owners * cap + rank.astype(jnp.int32)
    flags = (
        lax.broadcasted_iota(jnp.int32, (LANES, count), 0) - rope == of_request
    ).astype(jnp.float32).astype(jnp.bfloat16)

    group = 4
    part = group * cap
    lane = lax.broadcasted_iota(jnp.int32, (part, LANES), 1)
    flagged = (lane >= rope) & (lane < rope + req)

    def fill(owner_group):
        first = owner_group * part
        choose = (
            lax.broadcasted_iota(jnp.int32, (part, count), 0) + first == target
        ).astype(jnp.float32).astype(jnp.bfloat16)
        main = lax.dot_general(choose, renewed[:lat, :], NT, preferred_element_type=jnp.float32)
        tail = lax.dot_general(choose, renewed[lat:, :], NT, preferred_element_type=jnp.float32)
        mine = lax.dot_general(choose, flags, NT, preferred_element_type=jnp.float32)
        tail = jnp.where(flagged, 1.0 - mine, tail)
        send_rows[pl.ds(owner_group * group, group), :, :lat] = (
            main.astype(jnp.bfloat16).reshape(group, cap, lat)
        )
        send_rows[pl.ds(owner_group * group, group), :, lat:] = (
            tail.astype(jnp.bfloat16).reshape(group, cap, LANES)
        )

    def row_copy(step):
        peer = flip(me, order[step])
        return pltpu.make_async_remote_copy(
            src_ref=send_rows.at[peer],
            dst_ref=got_rows.at[step],
            send_sem=row_send.at[step],
            recv_sem=row_recv.at[step],
            device_id={"ep": peer},
            device_id_type=pl.DeviceIdType.MESH,
        )

    my_group = me // group
    seen = []
    for k in order + [0]:
        if k // group not in seen:
            seen.append(k // group)
    for index, bits in enumerate(seen):
        fill(flip(my_group, bits))
        if index == 0:
            pl.semaphore_wait(barrier, n - 1)
        for step, k in enumerate(order):
            if k // group == bits:
                row_copy(step).start()
    own_rows = pltpu.make_async_copy(send_rows.at[me], got_rows.at[n - 1], own_sem.at[0])
    own_rows.start()

    loads[0].wait()
    for r in range(req):
        halves, tails = [], []
        for q in range(qrows):
            turned = jnp.transpose(raw_queries[r, q].astype(jnp.float32))
            halves.append(turned[:, :lat].reshape(n, hpd, lat))
            tails.append(turned[:, lat:].reshape(n, hpd, rope))
        main = jnp.concatenate(halves, axis=1).reshape(rows_req, lat)
        tail = jnp.concatenate(tails, axis=1).reshape(rows_req, rope)
        extra = lax.broadcasted_iota(jnp.int32, (rows_req, LANES - rope), 1)
        tail = jnp.concatenate([tail, jnp.where(extra == r, MASKED, 0.0)], axis=1)
        queries[pl.ds(r * rows_req, rows_req), :lat] = main.astype(jnp.bfloat16)
        queries[pl.ds(r * rows_req, rows_req), lat:] = tail.astype(jnp.bfloat16)

    def absorb(where, scores, values, form, fresh):
        top = jnp.max(scores, axis=1, keepdims=True)
        if not fresh:
            was = highest[where, :1]
            top = jnp.maximum(top, was)
            keep = jnp.exp(was - top)
        weights = jnp.exp(scores - top)
        mass = jnp.sum(weights, axis=1, keepdims=True)
        blend = lax.dot_general(
            weights.astype(jnp.bfloat16), values, form, preferred_element_type=jnp.float32
        )
        if not fresh:
            mass = mass + denom[where, :1] * keep
            blend = blend + total[where, :] * keep
        highest[where, :] = jnp.broadcast_to(top, (top.shape[0], LANES))
        denom[where, :] = jnp.broadcast_to(mass, (top.shape[0], LANES))
        total[where, :] = blend

    for r in range(req):
        loads[1 + r].wait()
        where = pl.ds(r * rows_req, rows_req)
        limit = length_ref[r]

        def early(i, fresh):
            keys = old_rows[r, :, pl.ds(pl.multiple_of(i * chunk, chunk), chunk)]
            scores = scale * lax.dot_general(
                queries[where, :width], keys, NN, preferred_element_type=jnp.float32
            )
            position = i * chunk + lax.broadcasted_iota(jnp.int32, (rows_req, chunk), 1)
            scores = jnp.where(position < limit, scores, MASKED)
            absorb(where, scores, keys[:lat, :], NT, fresh)

        early(0, True)

        @pl.loop(1, old // chunk)
        def _(i):
            early(i, False)

    own_rows.wait()
    groups = [list(range(n - 1))[i : i + group] for i in range(0, n - 1, group)]
    for steps in groups:
        for step in steps:
            row_copy(step).wait_recv()
        first = steps[0]
        keys = got_rows[pl.ds(first, group)].reshape(part, lat + LANES)
        for r in range(req):
            where = pl.ds(r * rows_req, rows_req)
            scores = scale * lax.dot_general(
                queries[where, :], keys, NT, preferred_element_type=jnp.float32
            )
            absorb(where, scores, keys[:, :lat], NN, False)

    for r in range(req):
        where = pl.ds(r * rows_req, rows_req)
        latents[r] = (
            (total[where, :] / denom[where, :1]).astype(jnp.bfloat16).reshape(n, block, lat)
        )

    def latent_copy(step):
        peer = flip(me, order[step])
        return pltpu.make_async_remote_copy(
            src_ref=latents.at[:, peer],
            dst_ref=got_latents.at[step],
            send_sem=lat_send.at[step],
            recv_sem=lat_recv.at[step],
            device_id={"ep": peer},
            device_id_type=pl.DeviceIdType.MESH,
        )

    for step in range(n - 1):
        latent_copy(step).start()
    own_latents = pltpu.make_async_copy(latents.at[:, me], got_latents.at[n - 1], own_sem.at[1])
    own_latents.start()

    loads[1 + req].wait()
    for step in range(n - 1):
        row_copy(step).wait_send()
    own_latents.wait()
    rows = req * block
    head_of = lax.broadcasted_iota(jnp.int32, (group * rows, out_ref.shape[1]), 0) % hpd
    for steps in groups:
        for step in steps:
            latent_copy(step).wait_recv()
        left = got_latents[pl.ds(steps[0], group)].reshape(group * rows, lat)
        result = jnp.zeros(head_of.shape, jnp.float32)
        for h in range(hpd):
            value = jnp.dot(left, up[h], preferred_element_type=jnp.float32)
            result = jnp.where(head_of == h, value, result)
        result = result.astype(jnp.bfloat16)
        for i in range(group):
            step = steps[0] + i
            source = me if step == n - 1 else flip(me, order[step])
            out_ref[pl.ds(source * rows, rows), :] = result[i * rows : (i + 1) * rows]
    for step in range(n - 1):
        latent_copy(step).wait_send()


def fused(new_latent, latent_gain, row_slot, old_length, cache, queries, value_up):
    n = lax.axis_size("ep")
    req, cache_len, width = cache.shape
    lat = latent_gain.shape[0]
    count = new_latent.shape[0]
    cap = 2 * count // n
    qrows, heads = queries.shape[1:3]
    hpd, _, hd = value_up.shape
    scale = (hd + width - lat) ** (-0.5)
    old = cache_len // 2
    rows_req = qrows * heads
    block = qrows * hpd
    dims = (n, req, cache_len, width, lat, cap, heads, qrows, scale, min(512, old))
    bf16, f32 = jnp.bfloat16, jnp.float32
    vmem = pl.BlockSpec(memory_space=pltpu.VMEM)
    hbm = pl.BlockSpec(memory_space=pl.ANY)
    smem = pl.BlockSpec(memory_space=pltpu.SMEM)
    wide = lat + LANES
    out = pl.pallas_call(
        functools.partial(kernel, dims),
        out_shape=jax.ShapeDtypeStruct((n * req * block, hd), bf16),
        in_specs=[vmem, vmem, vmem, smem, hbm, hbm, hbm],
        out_specs=vmem,
        scratch_shapes=[
            pltpu.VMEM((wide, count), bf16),
            pltpu.VMEM((n, cap, wide), bf16),
            pltpu.VMEM((n, cap, wide), bf16),
            pltpu.VMEM((req, width, old), bf16),
            pltpu.VMEM((req * rows_req, wide), bf16),
            pltpu.VMEM((req, qrows, width, heads), bf16),
            pltpu.VMEM(value_up.shape, bf16),
            pltpu.VMEM((req * rows_req, lat), f32),
            pltpu.VMEM((req * rows_req, LANES), f32),
            pltpu.VMEM((req * rows_req, LANES), f32),
            pltpu.VMEM((req, n, block, lat), bf16),
            pltpu.VMEM((n, req, block, lat), bf16),
            pltpu.SemaphoreType.DMA((n,)),
            pltpu.SemaphoreType.DMA((n,)),
            pltpu.SemaphoreType.DMA((n,)),
            pltpu.SemaphoreType.DMA((n,)),
            pltpu.SemaphoreType.DMA((2,)),
            pltpu.SemaphoreType.DMA((req + 2,)),
        ],
        compiler_params=pltpu.CompilerParams(
            collective_id=0, has_side_effects=True, vmem_limit_bytes=48 * 1024 * 1024
        ),
        cost_estimate=pl.CostEstimate(
            flops=2 * req * rows_req * (old + n * cap) * (width + lat),
            bytes_accessed=2 * req * old * width,
            transcendentals=req * rows_req * (old + n * cap),
        ),
    )(
        new_latent.T,
        latent_gain[None, :],
        row_slot[None, :],
        old_length,
        jnp.swapaxes(cache, 1, 2),
        jnp.swapaxes(queries, 2, 3),
        value_up,
    )
    return out.reshape(n * req, qrows, hpd, hd)


def normalize(latent_rows, gains):
    widened = latent_rows.astype(jnp.float32)
    latent_width = gains.shape[0]
    latent_part = widened[:, :latent_width]
    factor = lax.rsqrt(jnp.mean(latent_part * latent_part, axis=1, keepdims=True) + 1e-06)
    return jnp.concatenate(
        [latent_part * factor * gains[None, :], widened[:, latent_width:]], axis=1
    ).astype(jnp.bfloat16)


def masked_scores(query_rows, key_rows, usable, score_scale):
    scores = (
        lax.dot_general(
            query_rows, key_rows, (((1,), (1,)), ((), ())), preferred_element_type=jnp.float32
        )
        * score_scale
    )
    return jnp.where(usable[None, :], scores, -1e30)


def collective(new_latent, latent_gain, row_slot, old_length, cache, queries, value_up):
    device_count = lax.axis_size("ep")
    req_count, cache_len, row_width = cache.shape
    latent_width = latent_gain.shape[0]
    row_count = new_latent.shape[0]
    capacity = 2 * row_count // device_count
    local_slots = req_count * cache_len
    query_count = queries.shape[1]
    head_count = queries.shape[2]
    score_scale = (value_up.shape[2] + row_width - latent_width) ** (-0.5)
    renewed = normalize(new_latent, latent_gain)
    owners = row_slot // local_slots
    belongs = (owners[:, None] == jnp.arange(device_count, dtype=jnp.int32)[None, :]).astype(
        jnp.int32
    )
    earlier = jnp.cumsum(belongs, axis=0) - belongs
    order_rank = jnp.sum(earlier * belongs, axis=1)
    target = owners * capacity + order_rank
    send_rows = (
        jnp.zeros((device_count * capacity, row_width), jnp.bfloat16).at[target].set(renewed)
    )
    send_rows = send_rows.reshape(device_count, capacity, row_width)
    send_slots = (
        jnp.full((device_count * capacity,), -1, jnp.int32)
        .at[target]
        .set(row_slot - owners * local_slots)
    )
    send_slots = send_slots.reshape(device_count, capacity)
    positions = jnp.arange(cache_len, dtype=jnp.int32)
    got_rows, got_slots = (
        lax.all_to_all(send_rows, "ep", split_axis=0, concat_axis=0, tiled=True),
        lax.all_to_all(send_slots, "ep", split_axis=0, concat_axis=0, tiled=True),
    )
    got_rows = got_rows.reshape(device_count * capacity, row_width)
    got_slots = got_slots.reshape(device_count * capacity)
    outputs = []
    old_len = cache_len // 2
    for request in range(req_count):
        query_rows = queries[request].reshape(query_count * head_count, row_width)
        old_rows = cache[request, :old_len]
        early_scores = masked_scores(
            query_rows, old_rows, positions[:old_len] < old_length[request], score_scale
        )
        owned = (got_slots >= 0) & (got_slots // cache_len == request)
        late_scores = masked_scores(query_rows, got_rows, owned, score_scale)
        highest = jnp.maximum(
            jnp.max(early_scores, axis=1, keepdims=True),
            jnp.max(late_scores, axis=1, keepdims=True),
        )
        early_weights = jnp.exp(early_scores - highest)
        late_weights = jnp.exp(late_scores - highest)
        denominator = jnp.sum(early_weights, axis=1, keepdims=True) + jnp.sum(
            late_weights, axis=1, keepdims=True
        )
        blended = jnp.dot(
            early_weights.astype(jnp.bfloat16), old_rows, preferred_element_type=jnp.float32
        )
        blended = blended + jnp.dot(
            late_weights.astype(jnp.bfloat16), got_rows, preferred_element_type=jnp.float32
        )
        blended = blended[:, :latent_width] / denominator
        outputs.append(blended.astype(jnp.bfloat16).reshape(query_count, head_count, latent_width))
    latent_out = jnp.stack(outputs, axis=0)
    return jnp.einsum(
        "rqhl,hld->rqhd",
        lax.all_to_all(latent_out, "ep", split_axis=2, concat_axis=0, tiled=True),
        value_up,
        preferred_element_type=jnp.float32,
    ).astype(jnp.bfloat16)


def local(*args):
    new_latent, latent_gain, _, _, cache, queries, value_up = args
    n = lax.axis_size("ep")
    lat = latent_gain.shape[0]
    rope = cache.shape[2] - lat
    whole_tiles = (
        n % 4 == 0
        and n & (n - 1) == 0
        and (2 * new_latent.shape[0] // n) % TILE == 0
        and (queries.shape[1] * value_up.shape[0]) % TILE == 0
        and value_up.shape[0] % 8 == 0
        and lat % LANES == 0
        and new_latent.shape[0] % LANES == 0
        and queries.shape[2] % LANES == 0
        and rope + cache.shape[0] <= LANES
    )
    return fused(*args) if whole_tiles else collective(*args)


def solution(mesh):
    in_specs = (
        P(("groups", "ep"), None),
        P(),
        P(("groups", "ep")),
        P(("groups", "ep")),
        P(("groups", "ep"), None, None),
        P(("groups", "ep"), None, None, None),
        P("ep", None, None),
    )
    out_specs = P("groups", None, "ep", None)
    return jax.shard_map(local, mesh=mesh, in_specs=in_specs, out_specs=out_specs, check_vma=False)
```

```python
import functools

import jax
import jax.numpy as jnp
from jax import lax
from jax.experimental import pallas as pl
from jax.experimental.pallas import tpu as pltpu
from jax.sharding import PartitionSpec as P

NN = (((1,), (0,)), ((), ()))
NT = (((1,), (1,)), ((), ()))
LANES = 128
TILE = 16
MASKED = -1e30


def flip(index, bits):
    out, place = index, 1
    while place <= bits:
        if bits & place:
            out = out + place * (1 - 2 * ((index // place) % 2))
        place *= 2
    return out


def kernel(
    dims,
    latent_hbm, gain_hbm, slot_hbm, length_hbm, cache_ref, query_ref, up_ref,
    out_ref,
    latent_ref, gain_ref, slot_ref, length_ref,
    renewed, send_rows, got_rows, old_rows, queries, raw_queries, up, total, highest, denom,
    latents, got_latents,
    row_send, row_recv, lat_send, lat_recv, own_sem, load_sem, small_sem,
):
    n, req, cache_len, width, lat, cap, heads, qrows, scale, chunk = dims
    me = lax.axis_index("ep")
    hpd = heads // n
    rope = width - lat
    old = cache_len // 2
    rows_req = qrows * heads
    block = qrows * hpd
    group = 4
    turns = list(range(n // group // 2, n // group)) + list(range(n // group // 2))[::-1]

    barrier = pltpu.get_barrier_semaphore()
    for k in range(1, n):
        pl.semaphore_signal(
            barrier, inc=1, device_id={"ep": flip(me, k)}, device_id_type=pl.DeviceIdType.MESH
        )

    smalls = [
        pltpu.make_async_copy(source, target, small_sem.at[i])
        for i, (source, target) in enumerate(
            [
                (latent_hbm, latent_ref),
                (slot_hbm, slot_ref),
                (gain_hbm, gain_ref),
                (length_hbm, length_ref),
            ]
        )
    ]
    for load in smalls:
        load.start()
    loads = [pltpu.make_async_copy(query_ref, raw_queries, load_sem.at[0])]
    for r in range(req):
        loads.append(
            pltpu.make_async_copy(
                cache_ref.at[r, :, pl.ds(0, old)], old_rows.at[r], load_sem.at[1 + r]
            )
        )
    loads.append(pltpu.make_async_copy(up_ref, up, load_sem.at[1 + req]))
    for load in loads:
        load.start()

    for load in smalls:
        load.wait()
    count = latent_ref.shape[1]
    wide = latent_ref[:lat, :].astype(jnp.float32)
    factor = lax.rsqrt(jnp.mean(wide * wide, axis=0, keepdims=True) + 1e-06)
    gains = jnp.transpose(jnp.broadcast_to(gain_ref[...], (LANES, lat)))
    gains = jnp.concatenate([gains] * (count // LANES), axis=1)
    renewed[:lat, :] = (wide * factor * gains).astype(jnp.bfloat16)
    renewed[lat:width, :] = latent_ref[lat:, :]
    renewed[width:, :] = jnp.zeros((lat + LANES - width, count), jnp.bfloat16)

    slots = slot_ref[...]
    owners = lax.div(slots, jnp.int32(req * cache_len))
    of_request = lax.div(slots - owners * (req * cache_len), jnp.int32(cache_len))
    belongs = (lax.broadcasted_iota(jnp.int32, (n, count), 0) == owners).astype(jnp.float32)
    before = (
        lax.broadcasted_iota(jnp.int32, (count, count), 0)
        < lax.broadcasted_iota(jnp.int32, (count, count), 1)
    ).astype(jnp.float32).astype(jnp.bfloat16)
    earlier = jnp.dot(belongs.astype(jnp.bfloat16), before, preferred_element_type=jnp.float32)
    rank = jnp.sum(earlier * belongs, axis=0, keepdims=True)
    target = owners * cap + rank.astype(jnp.int32)
    flags = (
        lax.broadcasted_iota(jnp.int32, (LANES, count), 0) - rope == of_request
    ).astype(jnp.float32).astype(jnp.bfloat16)

    part = group * cap
    lane = lax.broadcasted_iota(jnp.int32, (part, LANES), 1)
    flagged = (lane >= rope) & (lane < rope + req)

    def fill(owner_group):
        first = owner_group * part
        choose = (
            lax.broadcasted_iota(jnp.int32, (part, count), 0) + first == target
        ).astype(jnp.float32).astype(jnp.bfloat16)
        main = lax.dot_general(choose, renewed[:lat, :], NT, preferred_element_type=jnp.float32)
        tail = lax.dot_general(choose, renewed[lat:, :], NT, preferred_element_type=jnp.float32)
        mine = lax.dot_general(choose, flags, NT, preferred_element_type=jnp.float32)
        tail = jnp.where(flagged, 1.0 - mine, tail)
        send_rows[pl.ds(owner_group * group, group), :, :lat] = (
            main.astype(jnp.bfloat16).reshape(group, cap, lat)
        )
        send_rows[pl.ds(owner_group * group, group), :, lat:] = (
            tail.astype(jnp.bfloat16).reshape(group, cap, LANES)
        )

    def row_copy(step):
        peer = flip(me, step)
        return pltpu.make_async_remote_copy(
            src_ref=send_rows.at[peer],
            dst_ref=got_rows.at[step],
            send_sem=row_send.at[step],
            recv_sem=row_recv.at[step],
            device_id={"ep": peer},
            device_id_type=pl.DeviceIdType.MESH,
        )

    my_group = me // group
    for index, bits in enumerate(turns):
        fill(flip(my_group, bits))
        if index == 0:
            pl.semaphore_wait(barrier, n - 1)
        for step in range(max(bits * group, 1), (bits + 1) * group):
            row_copy(step).start()
    own_rows = pltpu.make_async_copy(send_rows.at[me], got_rows.at[0], own_sem.at[0])
    own_rows.start()

    loads[0].wait()
    for r in range(req):
        halves, tails = [], []
        for q in range(qrows):
            turned = jnp.transpose(raw_queries[r, q].astype(jnp.float32))
            halves.append(turned[:, :lat].reshape(n, hpd, lat))
            tails.append(turned[:, lat:].reshape(n, hpd, rope))
        main = jnp.concatenate(halves, axis=1).reshape(rows_req, lat)
        tail = jnp.concatenate(tails, axis=1).reshape(rows_req, rope)
        extra = lax.broadcasted_iota(jnp.int32, (rows_req, LANES - rope), 1)
        tail = jnp.concatenate([tail, jnp.where(extra == r, MASKED, 0.0)], axis=1)
        queries[pl.ds(r * rows_req, rows_req), :lat] = main.astype(jnp.bfloat16)
        queries[pl.ds(r * rows_req, rows_req), lat:] = tail.astype(jnp.bfloat16)

    def absorb(where, scores, values, form, fresh):
        top = jnp.max(scores, axis=1, keepdims=True)
        if not fresh:
            was = highest[where, :1]
            top = jnp.maximum(top, was)
            keep = jnp.exp(was - top)
        weights = jnp.exp(scores - top)
        mass = jnp.sum(weights, axis=1, keepdims=True)
        blend = lax.dot_general(
            weights.astype(jnp.bfloat16), values, form, preferred_element_type=jnp.float32
        )
        if not fresh:
            mass = mass + denom[where, :1] * keep
            blend = blend + total[where, :] * keep
        highest[where, :] = jnp.broadcast_to(top, (top.shape[0], LANES))
        denom[where, :] = jnp.broadcast_to(mass, (top.shape[0], LANES))
        total[where, :] = blend

    for r in range(req):
        loads[1 + r].wait()
        where = pl.ds(r * rows_req, rows_req)
        limit = length_ref[r]

        def early(i, fresh):
            keys = old_rows[r, :, pl.ds(pl.multiple_of(i * chunk, chunk), chunk)]
            scores = scale * lax.dot_general(
                queries[where, :width], keys, NN, preferred_element_type=jnp.float32
            )
            position = i * chunk + lax.broadcasted_iota(jnp.int32, (rows_req, chunk), 1)
            scores = jnp.where(position < limit, scores, MASKED)
            absorb(where, scores, keys[:lat, :], NT, fresh)

        early(0, True)

        @pl.loop(1, old // chunk)
        def _(i):
            early(i, False)

    own_rows.wait()
    for first in range(0, n, group):
        for step in range(max(first, 1), first + group):
            row_copy(step).wait_recv()
        keys = got_rows[pl.ds(first, group)].reshape(part, lat + LANES)
        for r in range(req):
            where = pl.ds(r * rows_req, rows_req)
            scores = scale * lax.dot_general(
                queries[where, :], keys, NT, preferred_element_type=jnp.float32
            )
            absorb(where, scores, keys[:, :lat], NN, False)

    for r in range(req):
        where = pl.ds(r * rows_req, rows_req)
        latents[r] = (
            (total[where, :] / denom[where, :1]).astype(jnp.bfloat16).reshape(n, block, lat)
        )

    def latent_copy(step):
        peer = flip(me, step)
        return pltpu.make_async_remote_copy(
            src_ref=latents.at[:, peer],
            dst_ref=got_latents.at[step],
            send_sem=lat_send.at[step],
            recv_sem=lat_recv.at[step],
            device_id={"ep": peer},
            device_id_type=pl.DeviceIdType.MESH,
        )

    for bits in turns:
        for step in range(max(bits * group, 1), (bits + 1) * group):
            latent_copy(step).start()
    own_latents = pltpu.make_async_copy(latents.at[:, me], got_latents.at[0], own_sem.at[1])
    own_latents.start()

    loads[1 + req].wait()
    for step in range(1, n):
        row_copy(step).wait_send()
    own_latents.wait()
    rows = req * block
    head_of = lax.broadcasted_iota(jnp.int32, (group * rows, out_ref.shape[1]), 0) % hpd
    for first in range(0, n, group):
        for step in range(max(first, 1), first + group):
            latent_copy(step).wait_recv()
        left = got_latents[pl.ds(first, group)].reshape(group * rows, lat)
        result = jnp.zeros(head_of.shape, jnp.float32)
        for h in range(hpd):
            value = jnp.dot(left, up[h], preferred_element_type=jnp.float32)
            result = jnp.where(head_of == h, value, result)
        result = result.astype(jnp.bfloat16)
        for i in range(group):
            source = flip(me, first + i)
            out_ref[pl.ds(source * rows, rows), :] = result[i * rows : (i + 1) * rows]
    for step in range(1, n):
        latent_copy(step).wait_send()


def fused(new_latent, latent_gain, row_slot, old_length, cache, queries, value_up):
    n = lax.axis_size("ep")
    req, cache_len, width = cache.shape
    lat = latent_gain.shape[0]
    count = new_latent.shape[0]
    cap = 2 * count // n
    qrows, heads = queries.shape[1:3]
    hpd, _, hd = value_up.shape
    scale = (hd + width - lat) ** (-0.5)
    old = cache_len // 2
    rows_req = qrows * heads
    block = qrows * hpd
    dims = (n, req, cache_len, width, lat, cap, heads, qrows, scale, min(512, old))
    bf16, f32 = jnp.bfloat16, jnp.float32
    vmem = pl.BlockSpec(memory_space=pltpu.VMEM)
    hbm = pl.BlockSpec(memory_space=pl.ANY)
    wide = lat + LANES
    out = pl.pallas_call(
        functools.partial(kernel, dims),
        out_shape=jax.ShapeDtypeStruct((n * req * block, hd), bf16),
        in_specs=[hbm] * 7,
        out_specs=vmem,
        scratch_shapes=[
            pltpu.VMEM((width, count), bf16),
            pltpu.VMEM((1, lat), f32),
            pltpu.VMEM((1, count), jnp.int32),
            pltpu.SMEM((req,), jnp.int32),
            pltpu.VMEM((wide, count), bf16),
            pltpu.VMEM((n, cap, wide), bf16),
            pltpu.VMEM((n, cap, wide), bf16),
            pltpu.VMEM((req, width, old), bf16),
            pltpu.VMEM((req * rows_req, wide), bf16),
            pltpu.VMEM((req, qrows, width, heads), bf16),
            pltpu.VMEM(value_up.shape, bf16),
            pltpu.VMEM((req * rows_req, lat), f32),
            pltpu.VMEM((req * rows_req, LANES), f32),
            pltpu.VMEM((req * rows_req, LANES), f32),
            pltpu.VMEM((req, n, block, lat), bf16),
            pltpu.VMEM((n, req, block, lat), bf16),
            pltpu.SemaphoreType.DMA((n,)),
            pltpu.SemaphoreType.DMA((n,)),
            pltpu.SemaphoreType.DMA((n,)),
            pltpu.SemaphoreType.DMA((n,)),
            pltpu.SemaphoreType.DMA((2,)),
            pltpu.SemaphoreType.DMA((req + 2,)),
            pltpu.SemaphoreType.DMA((4,)),
        ],
        compiler_params=pltpu.CompilerParams(
            collective_id=0, has_side_effects=True, vmem_limit_bytes=63 * 1024 * 1024
        ),
        cost_estimate=pl.CostEstimate(
            flops=2 * req * rows_req * (old + n * cap) * (width + lat),
            bytes_accessed=2 * req * old * width,
            transcendentals=req * rows_req * (old + n * cap),
        ),
    )(
        new_latent.T,
        latent_gain[None, :],
        row_slot[None, :],
        old_length,
        jnp.swapaxes(cache, 1, 2),
        jnp.swapaxes(queries, 2, 3),
        value_up,
    )
    return out.reshape(n * req, qrows, hpd, hd)


def normalize(latent_rows, gains):
    widened = latent_rows.astype(jnp.float32)
    latent_width = gains.shape[0]
    latent_part = widened[:, :latent_width]
    factor = lax.rsqrt(jnp.mean(latent_part * latent_part, axis=1, keepdims=True) + 1e-06)
    return jnp.concatenate(
        [latent_part * factor * gains[None, :], widened[:, latent_width:]], axis=1
    ).astype(jnp.bfloat16)


def masked_scores(query_rows, key_rows, usable, score_scale):
    scores = (
        lax.dot_general(
            query_rows, key_rows, (((1,), (1,)), ((), ())), preferred_element_type=jnp.float32
        )
        * score_scale
    )
    return jnp.where(usable[None, :], scores, -1e30)


def collective(new_latent, latent_gain, row_slot, old_length, cache, queries, value_up):
    device_count = lax.axis_size("ep")
    req_count, cache_len, row_width = cache.shape
    latent_width = latent_gain.shape[0]
    row_count = new_latent.shape[0]
    capacity = 2 * row_count // device_count
    local_slots = req_count * cache_len
    query_count = queries.shape[1]
    head_count = queries.shape[2]
    score_scale = (value_up.shape[2] + row_width - latent_width) ** (-0.5)
    renewed = normalize(new_latent, latent_gain)
    owners = row_slot // local_slots
    belongs = (owners[:, None] == jnp.arange(device_count, dtype=jnp.int32)[None, :]).astype(
        jnp.int32
    )
    earlier = jnp.cumsum(belongs, axis=0) - belongs
    order_rank = jnp.sum(earlier * belongs, axis=1)
    target = owners * capacity + order_rank
    send_rows = (
        jnp.zeros((device_count * capacity, row_width), jnp.bfloat16).at[target].set(renewed)
    )
    send_rows = send_rows.reshape(device_count, capacity, row_width)
    send_slots = (
        jnp.full((device_count * capacity,), -1, jnp.int32)
        .at[target]
        .set(row_slot - owners * local_slots)
    )
    send_slots = send_slots.reshape(device_count, capacity)
    positions = jnp.arange(cache_len, dtype=jnp.int32)
    got_rows, got_slots = (
        lax.all_to_all(send_rows, "ep", split_axis=0, concat_axis=0, tiled=True),
        lax.all_to_all(send_slots, "ep", split_axis=0, concat_axis=0, tiled=True),
    )
    got_rows = got_rows.reshape(device_count * capacity, row_width)
    got_slots = got_slots.reshape(device_count * capacity)
    outputs = []
    old_len = cache_len // 2
    for request in range(req_count):
        query_rows = queries[request].reshape(query_count * head_count, row_width)
        old_rows = cache[request, :old_len]
        early_scores = masked_scores(
            query_rows, old_rows, positions[:old_len] < old_length[request], score_scale
        )
        owned = (got_slots >= 0) & (got_slots // cache_len == request)
        late_scores = masked_scores(query_rows, got_rows, owned, score_scale)
        highest = jnp.maximum(
            jnp.max(early_scores, axis=1, keepdims=True),
            jnp.max(late_scores, axis=1, keepdims=True),
        )
        early_weights = jnp.exp(early_scores - highest)
        late_weights = jnp.exp(late_scores - highest)
        denominator = jnp.sum(early_weights, axis=1, keepdims=True) + jnp.sum(
            late_weights, axis=1, keepdims=True
        )
        blended = jnp.dot(
            early_weights.astype(jnp.bfloat16), old_rows, preferred_element_type=jnp.float32
        )
        blended = blended + jnp.dot(
            late_weights.astype(jnp.bfloat16), got_rows, preferred_element_type=jnp.float32
        )
        blended = blended[:, :latent_width] / denominator
        outputs.append(blended.astype(jnp.bfloat16).reshape(query_count, head_count, latent_width))
    latent_out = jnp.stack(outputs, axis=0)
    return jnp.einsum(
        "rqhl,hld->rqhd",
        lax.all_to_all(latent_out, "ep", split_axis=2, concat_axis=0, tiled=True),
        value_up,
        preferred_element_type=jnp.float32,
    ).astype(jnp.bfloat16)


def local(*args):
    new_latent, latent_gain, _, _, cache, queries, value_up = args
    n = lax.axis_size("ep")
    lat = latent_gain.shape[0]
    rope = cache.shape[2] - lat
    whole_tiles = (
        n % 4 == 0
        and n & (n - 1) == 0
        and (2 * new_latent.shape[0] // n) % TILE == 0
        and (queries.shape[1] * value_up.shape[0]) % TILE == 0
        and value_up.shape[0] % 8 == 0
        and lat % LANES == 0
        and new_latent.shape[0] % LANES == 0
        and queries.shape[2] % LANES == 0
        and rope + cache.shape[0] <= LANES
    )
    return fused(*args) if whole_tiles else collective(*args)


def solution(mesh):
    in_specs = (
        P(("groups", "ep"), None),
        P(),
        P(("groups", "ep")),
        P(("groups", "ep")),
        P(("groups", "ep"), None, None),
        P(("groups", "ep"), None, None, None),
        P("ep", None, None),
    )
    out_specs = P("groups", None, "ep", None)
    return jax.shard_map(local, mesh=mesh, in_specs=in_specs, out_specs=out_specs, check_vma=False)
```

```python
import functools

import jax
import jax.numpy as jnp
from jax import lax
from jax.experimental import pallas as pl
from jax.experimental.pallas import tpu as pltpu
from jax.sharding import PartitionSpec as P

NN = (((1,), (0,)), ((), ()))
NT = (((1,), (1,)), ((), ()))
LANES = 128
TILE = 16
MASKED = -1e30


def flip(index, bits):
    out, place = index, 1
    while place <= bits:
        if bits & place:
            out = out + place * (1 - 2 * ((index // place) % 2))
        place *= 2
    return out


def kernel(
    dims,
    latent_hbm, gain_hbm, slot_hbm, length_hbm, cache_ref, query_ref, up_ref,
    out_ref,
    latent_ref, gain_ref, slot_ref, length_ref,
    renewed, send_rows, got_rows, send_tails, got_tails, send_marks, got_marks, old_rows, queries, raw_queries, up, total, highest, denom,
    latents, got_latents,
    row_send, row_recv, lat_send, lat_recv, own_sem, load_sem, small_sem,
):
    n, req, cache_len, width, lat, cap, heads, qrows, scale, chunk = dims
    me = lax.axis_index("ep")
    hpd = heads // n
    rope = width - lat
    old = cache_len // 2
    rows_req = qrows * heads
    block = qrows * hpd
    group = 4
    turns = list(range(n // group // 2, n // group)) + list(range(n // group // 2))[::-1]

    barrier = pltpu.get_barrier_semaphore()
    for k in range(1, n):
        pl.semaphore_signal(
            barrier, inc=1, device_id={"ep": flip(me, k)}, device_id_type=pl.DeviceIdType.MESH
        )

    smalls = [
        pltpu.make_async_copy(source, target, small_sem.at[i])
        for i, (source, target) in enumerate(
            [
                (latent_hbm, latent_ref),
                (slot_hbm, slot_ref),
                (gain_hbm, gain_ref),
                (length_hbm, length_ref),
            ]
        )
    ]
    for load in smalls:
        load.start()
    loads = [pltpu.make_async_copy(query_ref, raw_queries, load_sem.at[0])]
    for r in range(req):
        loads.append(
            pltpu.make_async_copy(
                cache_ref.at[r, :, pl.ds(0, old)], old_rows.at[r], load_sem.at[1 + r]
            )
        )
    loads.append(pltpu.make_async_copy(up_ref, up, load_sem.at[1 + req]))
    for load in loads:
        load.start()

    for load in smalls:
        load.wait()
    count = latent_ref.shape[1]
    wide = latent_ref[:lat, :].astype(jnp.float32)
    factor = lax.rsqrt(jnp.mean(wide * wide, axis=0, keepdims=True) + 1e-06)
    gains = jnp.transpose(jnp.broadcast_to(gain_ref[...], (LANES, lat)))
    gains = jnp.concatenate([gains] * (count // LANES), axis=1)
    renewed[:lat, :] = (wide * factor * gains).astype(jnp.bfloat16)
    renewed[lat:width, :] = latent_ref[lat:, :]
    renewed[width:, :] = jnp.zeros((lat + LANES - width, count), jnp.bfloat16)

    slots = slot_ref[...]
    owners = lax.div(slots, jnp.int32(req * cache_len))
    of_request = lax.div(slots - owners * (req * cache_len), jnp.int32(cache_len))
    belongs = (lax.broadcasted_iota(jnp.int32, (n, count), 0) == owners).astype(jnp.float32)
    before = (
        lax.broadcasted_iota(jnp.int32, (count, count), 0)
        < lax.broadcasted_iota(jnp.int32, (count, count), 1)
    ).astype(jnp.float32).astype(jnp.bfloat16)
    earlier = jnp.dot(belongs.astype(jnp.bfloat16), before, preferred_element_type=jnp.float32)
    rank = jnp.sum(earlier * belongs, axis=0, keepdims=True)
    target = owners * cap + rank.astype(jnp.int32)
    part = group * cap
    half = cap // 2
    marks = jnp.broadcast_to((of_request + 1).astype(jnp.float32), (TILE, count))
    marks = marks.astype(jnp.bfloat16)

    def swap(packed):
        return jnp.concatenate([packed[..., rope:], packed[..., :rope]], axis=-1)

    def fill(owner_group):
        first = owner_group * part
        choose = (
            lax.broadcasted_iota(jnp.int32, (part, count), 0) + first == target
        ).astype(jnp.float32).astype(jnp.bfloat16)
        main = lax.dot_general(choose, renewed[:lat, :], NT, preferred_element_type=jnp.float32)
        tail = lax.dot_general(choose, renewed[lat:, :], NT, preferred_element_type=jnp.float32)
        mark = lax.dot_general(marks, choose, NT, preferred_element_type=jnp.float32)
        where = pl.ds(owner_group * group, group)
        send_rows[where] = main.astype(jnp.bfloat16).reshape(group, cap, lat)
        tail = tail.reshape(group, cap, LANES)
        send_tails[where] = (tail[:, :half] + swap(tail[:, half:])).astype(jnp.bfloat16)
        for i in range(group):
            one = mark[:1, i * cap : (i + 1) * cap]
            send_marks[owner_group * group + i] = jnp.concatenate([one, one], axis=1)

    class Several:
        def __init__(self, copies):
            self.copies = copies

        def start(self):
            for copy in self.copies:
                copy.start()

        def wait(self):
            for copy in self.copies:
                copy.wait()

        def wait_send(self):
            for copy in self.copies:
                copy.wait_send()

        def wait_recv(self):
            for copy in self.copies:
                copy.wait_recv()

    pairs = [(send_marks, got_marks), (send_tails, got_tails), (send_rows, got_rows)]

    def row_copy(step):
        peer = flip(me, step)
        return Several(
            [
                pltpu.make_async_remote_copy(
                    src_ref=sent.at[peer],
                    dst_ref=got.at[step],
                    send_sem=row_send.at[i, step],
                    recv_sem=row_recv.at[i, step],
                    device_id={"ep": peer},
                    device_id_type=pl.DeviceIdType.MESH,
                )
                for i, (sent, got) in enumerate(pairs)
            ]
        )

    my_group = me // group
    for index, bits in enumerate(turns):
        fill(flip(my_group, bits))
        if index == 0:
            pl.semaphore_wait(barrier, n - 1)
        for step in range(max(bits * group, 1), (bits + 1) * group):
            row_copy(step).start()
    own_rows = Several(
        [
            pltpu.make_async_copy(sent.at[me], got.at[0], own_sem.at[1 + i])
            for i, (sent, got) in enumerate(pairs)
        ]
    )
    own_rows.start()

    loads[0].wait()
    for r in range(req):
        halves, tails = [], []
        for q in range(qrows):
            turned = jnp.transpose(raw_queries[r, q].astype(jnp.float32))
            halves.append(turned[:, :lat].reshape(n, hpd, lat))
            tails.append(turned[:, lat:].reshape(n, hpd, rope))
        main = jnp.concatenate(halves, axis=1).reshape(rows_req, lat)
        tail = jnp.concatenate(tails, axis=1).reshape(rows_req, rope)
        tail = jnp.concatenate([tail, jnp.zeros((rows_req, LANES - rope), jnp.float32)], axis=1)
        queries[pl.ds(r * rows_req, rows_req), :lat] = main.astype(jnp.bfloat16)
        queries[pl.ds(r * rows_req, rows_req), lat:] = tail.astype(jnp.bfloat16)

    def absorb(where, scores, values, form, fresh):
        top = jnp.max(scores, axis=1, keepdims=True)
        if not fresh:
            was = highest[where, :1]
            top = jnp.maximum(top, was)
            keep = jnp.exp(was - top)
        weights = jnp.exp(scores - top)
        mass = jnp.sum(weights, axis=1, keepdims=True)
        blend = lax.dot_general(
            weights.astype(jnp.bfloat16), values, form, preferred_element_type=jnp.float32
        )
        if not fresh:
            mass = mass + denom[where, :1] * keep
            blend = blend + total[where, :] * keep
        highest[where, :] = jnp.broadcast_to(top, (top.shape[0], LANES))
        denom[where, :] = jnp.broadcast_to(mass, (top.shape[0], LANES))
        total[where, :] = blend

    for r in range(req):
        loads[1 + r].wait()
        where = pl.ds(r * rows_req, rows_req)
        limit = length_ref[r]

        def early(i, fresh):
            keys = old_rows[r, :, pl.ds(pl.multiple_of(i * chunk, chunk), chunk)]
            scores = scale * lax.dot_general(
                queries[where, :width], keys, NN, preferred_element_type=jnp.float32
            )
            position = i * chunk + lax.broadcasted_iota(jnp.int32, (rows_req, chunk), 1)
            scores = jnp.where(position < limit, scores, MASKED)
            absorb(where, scores, keys[:lat, :], NT, fresh)

        early(0, True)

        @pl.loop(1, old // chunk)
        def _(i):
            early(i, False)

    own_rows.wait()
    for first in range(0, n, group):
        for step in range(max(first, 1), first + group):
            row_copy(step).wait_recv()
        packed = got_tails[pl.ds(first, group)].astype(jnp.float32)
        tail = jnp.concatenate([packed, swap(packed)], axis=1).astype(jnp.bfloat16)
        values = got_rows[pl.ds(first, group)].reshape(part, lat)
        keys = jnp.concatenate([values, tail.reshape(part, LANES)], axis=1)
        low = lax.broadcasted_iota(jnp.int32, (1, LANES), 1) < cap
        mark = jnp.concatenate(
            [
                jnp.where(low, got_marks[first + i], got_marks[first + i + 1])
                for i in range(0, group, 2)
            ],
            axis=1,
        )
        for r in range(req):
            where = pl.ds(r * rows_req, rows_req)
            scores = scale * lax.dot_general(
                queries[where, :], keys, NT, preferred_element_type=jnp.float32
            )
            scores = jnp.where(mark == r + 1.0, scores, MASKED)
            absorb(where, scores, values, NN, False)

    for r in range(req):
        where = pl.ds(r * rows_req, rows_req)
        latents[r] = (
            (total[where, :] / denom[where, :1]).astype(jnp.bfloat16).reshape(n, block, lat)
        )

    def latent_copy(step):
        peer = flip(me, step)
        return pltpu.make_async_remote_copy(
            src_ref=latents.at[:, peer],
            dst_ref=got_latents.at[step],
            send_sem=lat_send.at[step],
            recv_sem=lat_recv.at[step],
            device_id={"ep": peer},
            device_id_type=pl.DeviceIdType.MESH,
        )

    for bits in turns:
        for step in range(max(bits * group, 1), (bits + 1) * group):
            latent_copy(step).start()
    own_latents = pltpu.make_async_copy(latents.at[:, me], got_latents.at[0], own_sem.at[0])
    own_latents.start()

    loads[1 + req].wait()
    for step in range(1, n):
        row_copy(step).wait_send()
    own_latents.wait()
    rows = req * block
    head_of = lax.broadcasted_iota(jnp.int32, (group * rows, out_ref.shape[1]), 0) % hpd
    for first in range(0, n, group):
        for step in range(max(first, 1), first + group):
            latent_copy(step).wait_recv()
        left = got_latents[pl.ds(first, group)].reshape(group * rows, lat)
        result = jnp.zeros(head_of.shape, jnp.float32)
        for h in range(hpd):
            value = jnp.dot(left, up[h], preferred_element_type=jnp.float32)
            result = jnp.where(head_of == h, value, result)
        result = result.astype(jnp.bfloat16)
        for i in range(group):
            source = flip(me, first + i)
            out_ref[pl.ds(source * rows, rows), :] = result[i * rows : (i + 1) * rows]
    for step in range(1, n):
        latent_copy(step).wait_send()


def fused(new_latent, latent_gain, row_slot, old_length, cache, queries, value_up):
    n = lax.axis_size("ep")
    req, cache_len, width = cache.shape
    lat = latent_gain.shape[0]
    count = new_latent.shape[0]
    cap = 2 * count // n
    qrows, heads = queries.shape[1:3]
    hpd, _, hd = value_up.shape
    scale = (hd + width - lat) ** (-0.5)
    old = cache_len // 2
    rows_req = qrows * heads
    block = qrows * hpd
    dims = (n, req, cache_len, width, lat, cap, heads, qrows, scale, min(512, old))
    bf16, f32 = jnp.bfloat16, jnp.float32
    vmem = pl.BlockSpec(memory_space=pltpu.VMEM)
    hbm = pl.BlockSpec(memory_space=pl.ANY)
    wide = lat + LANES
    out = pl.pallas_call(
        functools.partial(kernel, dims),
        out_shape=jax.ShapeDtypeStruct((n * req * block, hd), bf16),
        in_specs=[hbm] * 7,
        out_specs=vmem,
        scratch_shapes=[
            pltpu.VMEM((width, count), bf16),
            pltpu.VMEM((1, lat), f32),
            pltpu.VMEM((1, count), jnp.int32),
            pltpu.SMEM((req,), jnp.int32),
            pltpu.VMEM((wide, count), bf16),
            pltpu.VMEM((n, cap, lat), bf16),
            pltpu.VMEM((n, cap, lat), bf16),
            pltpu.VMEM((n, cap // 2, LANES), bf16),
            pltpu.VMEM((n, cap // 2, LANES), bf16),
            pltpu.VMEM((n, 1, LANES), f32),
            pltpu.VMEM((n, 1, LANES), f32),
            pltpu.VMEM((req, width, old), bf16),
            pltpu.VMEM((req * rows_req, wide), bf16),
            pltpu.VMEM((req, qrows, width, heads), bf16),
            pltpu.VMEM(value_up.shape, bf16),
            pltpu.VMEM((req * rows_req, lat), f32),
            pltpu.VMEM((req * rows_req, LANES), f32),
            pltpu.VMEM((req * rows_req, LANES), f32),
            pltpu.VMEM((req, n, block, lat), bf16),
            pltpu.VMEM((n, req, block, lat), bf16),
            pltpu.SemaphoreType.DMA((3, n)),
            pltpu.SemaphoreType.DMA((3, n)),
            pltpu.SemaphoreType.DMA((n,)),
            pltpu.SemaphoreType.DMA((n,)),
            pltpu.SemaphoreType.DMA((4,)),
            pltpu.SemaphoreType.DMA((req + 2,)),
            pltpu.SemaphoreType.DMA((4,)),
        ],
        compiler_params=pltpu.CompilerParams(
            collective_id=0, has_side_effects=True, vmem_limit_bytes=63 * 1024 * 1024
        ),
        cost_estimate=pl.CostEstimate(
            flops=2 * req * rows_req * (old + n * cap) * (width + lat),
            bytes_accessed=2 * req * old * width,
            transcendentals=req * rows_req * (old + n * cap),
        ),
    )(
        new_latent.T,
        latent_gain[None, :],
        row_slot[None, :],
        old_length,
        jnp.swapaxes(cache, 1, 2),
        jnp.swapaxes(queries, 2, 3),
        value_up,
    )
    return out.reshape(n * req, qrows, hpd, hd)


def normalize(latent_rows, gains):
    widened = latent_rows.astype(jnp.float32)
    latent_width = gains.shape[0]
    latent_part = widened[:, :latent_width]
    factor = lax.rsqrt(jnp.mean(latent_part * latent_part, axis=1, keepdims=True) + 1e-06)
    return jnp.concatenate(
        [latent_part * factor * gains[None, :], widened[:, latent_width:]], axis=1
    ).astype(jnp.bfloat16)


def masked_scores(query_rows, key_rows, usable, score_scale):
    scores = (
        lax.dot_general(
            query_rows, key_rows, (((1,), (1,)), ((), ())), preferred_element_type=jnp.float32
        )
        * score_scale
    )
    return jnp.where(usable[None, :], scores, -1e30)


def collective(new_latent, latent_gain, row_slot, old_length, cache, queries, value_up):
    device_count = lax.axis_size("ep")
    req_count, cache_len, row_width = cache.shape
    latent_width = latent_gain.shape[0]
    row_count = new_latent.shape[0]
    capacity = 2 * row_count // device_count
    local_slots = req_count * cache_len
    query_count = queries.shape[1]
    head_count = queries.shape[2]
    score_scale = (value_up.shape[2] + row_width - latent_width) ** (-0.5)
    renewed = normalize(new_latent, latent_gain)
    owners = row_slot // local_slots
    belongs = (owners[:, None] == jnp.arange(device_count, dtype=jnp.int32)[None, :]).astype(
        jnp.int32
    )
    earlier = jnp.cumsum(belongs, axis=0) - belongs
    order_rank = jnp.sum(earlier * belongs, axis=1)
    target = owners * capacity + order_rank
    send_rows = (
        jnp.zeros((device_count * capacity, row_width), jnp.bfloat16).at[target].set(renewed)
    )
    send_rows = send_rows.reshape(device_count, capacity, row_width)
    send_slots = (
        jnp.full((device_count * capacity,), -1, jnp.int32)
        .at[target]
        .set(row_slot - owners * local_slots)
    )
    send_slots = send_slots.reshape(device_count, capacity)
    positions = jnp.arange(cache_len, dtype=jnp.int32)
    got_rows, got_slots = (
        lax.all_to_all(send_rows, "ep", split_axis=0, concat_axis=0, tiled=True),
        lax.all_to_all(send_slots, "ep", split_axis=0, concat_axis=0, tiled=True),
    )
    got_rows = got_rows.reshape(device_count * capacity, row_width)
    got_slots = got_slots.reshape(device_count * capacity)
    outputs = []
    old_len = cache_len // 2
    for request in range(req_count):
        query_rows = queries[request].reshape(query_count * head_count, row_width)
        old_rows = cache[request, :old_len]
        early_scores = masked_scores(
            query_rows, old_rows, positions[:old_len] < old_length[request], score_scale
        )
        owned = (got_slots >= 0) & (got_slots // cache_len == request)
        late_scores = masked_scores(query_rows, got_rows, owned, score_scale)
        highest = jnp.maximum(
            jnp.max(early_scores, axis=1, keepdims=True),
            jnp.max(late_scores, axis=1, keepdims=True),
        )
        early_weights = jnp.exp(early_scores - highest)
        late_weights = jnp.exp(late_scores - highest)
        denominator = jnp.sum(early_weights, axis=1, keepdims=True) + jnp.sum(
            late_weights, axis=1, keepdims=True
        )
        blended = jnp.dot(
            early_weights.astype(jnp.bfloat16), old_rows, preferred_element_type=jnp.float32
        )
        blended = blended + jnp.dot(
            late_weights.astype(jnp.bfloat16), got_rows, preferred_element_type=jnp.float32
        )
        blended = blended[:, :latent_width] / denominator
        outputs.append(blended.astype(jnp.bfloat16).reshape(query_count, head_count, latent_width))
    latent_out = jnp.stack(outputs, axis=0)
    return jnp.einsum(
        "rqhl,hld->rqhd",
        lax.all_to_all(latent_out, "ep", split_axis=2, concat_axis=0, tiled=True),
        value_up,
        preferred_element_type=jnp.float32,
    ).astype(jnp.bfloat16)


def local(*args):
    new_latent, latent_gain, _, _, cache, queries, value_up = args
    n = lax.axis_size("ep")
    lat = latent_gain.shape[0]
    rope = cache.shape[2] - lat
    whole_tiles = (
        n % 4 == 0
        and n & (n - 1) == 0
        and 4 * new_latent.shape[0] // n == LANES
        and (queries.shape[1] * value_up.shape[0]) % TILE == 0
        and value_up.shape[0] % 8 == 0
        and lat % LANES == 0
        and new_latent.shape[0] % LANES == 0
        and queries.shape[2] % LANES == 0
        and 2 * rope == LANES
    )
    return fused(*args) if whole_tiles else collective(*args)


def solution(mesh):
    in_specs = (
        P(("groups", "ep"), None),
        P(),
        P(("groups", "ep")),
        P(("groups", "ep")),
        P(("groups", "ep"), None, None),
        P(("groups", "ep"), None, None, None),
        P("ep", None, None),
    )
    out_specs = P("groups", None, "ep", None)
    return jax.shard_map(local, mesh=mesh, in_specs=in_specs, out_specs=out_specs, check_vma=False)
```

```python
import functools

import jax
import jax.numpy as jnp
from jax import lax
from jax.experimental import pallas as pl
from jax.experimental.pallas import tpu as pltpu
from jax.sharding import PartitionSpec as P

NN = (((1,), (0,)), ((), ()))
NT = (((1,), (1,)), ((), ()))
LANES = 128
TILE = 16
MASKED = -1e30


def flip(index, bits):
    out, place = index, 1
    while place <= bits:
        if bits & place:
            out = out + place * (1 - 2 * ((index // place) % 2))
        place *= 2
    return out


def kernel(
    dims,
    latent_hbm, gain_hbm, slot_hbm, length_hbm, cache_ref, query_ref, up_ref,
    out_ref,
    latent_ref, gain_ref, slot_ref, length_ref,
    renewed, send_rows, got_rows, send_tails, got_tails, send_marks, got_marks, old_rows, queries, raw_queries, up, total, highest, denom,
    latents, got_latents,
    row_send, row_recv, lat_send, lat_recv, own_sem, load_sem, small_sem,
):
    n, req, cache_len, width, lat, cap, heads, qrows, scale, chunk = dims
    me = lax.axis_index("ep")
    hpd = heads // n
    rope = width - lat
    old = cache_len // 2
    rows_req = qrows * heads
    block = qrows * hpd
    group = 4
    turns = list(range(n // group // 2, n // group)) + list(range(n // group // 2))[::-1]

    smalls = [
        pltpu.make_async_copy(source, target, small_sem.at[i])
        for i, (source, target) in enumerate(
            [
                (latent_hbm, latent_ref),
                (slot_hbm, slot_ref),
                (gain_hbm, gain_ref),
                (length_hbm, length_ref),
            ]
        )
    ]
    for load in smalls:
        load.start()

    barrier = pltpu.get_barrier_semaphore()
    for k in range(1, n):
        pl.semaphore_signal(
            barrier, inc=1, device_id={"ep": flip(me, k)}, device_id_type=pl.DeviceIdType.MESH
        )

    loads = [pltpu.make_async_copy(query_ref, raw_queries, load_sem.at[0])]
    for r in range(req):
        loads.append(
            pltpu.make_async_copy(
                cache_ref.at[r, :, pl.ds(0, old)], old_rows.at[r], load_sem.at[1 + r]
            )
        )
    loads.append(pltpu.make_async_copy(up_ref, up, load_sem.at[1 + req]))
    for load in loads:
        load.start()

    count = latent_ref.shape[1]
    before = (
        lax.broadcasted_iota(jnp.int32, (count, count), 0)
        < lax.broadcasted_iota(jnp.int32, (count, count), 1)
    ).astype(jnp.float32).astype(jnp.bfloat16)
    smalls[1].wait()
    slots = slot_ref[...]
    owners = lax.div(slots, jnp.int32(req * cache_len))
    of_request = lax.div(slots - owners * (req * cache_len), jnp.int32(cache_len))
    belongs = (lax.broadcasted_iota(jnp.int32, (n, count), 0) == owners).astype(jnp.float32)
    earlier = jnp.dot(belongs.astype(jnp.bfloat16), before, preferred_element_type=jnp.float32)
    rank = jnp.sum(earlier * belongs, axis=0, keepdims=True)
    target = owners * cap + rank.astype(jnp.int32)
    part = group * cap
    half = cap // 2
    marks = jnp.broadcast_to((of_request + 1).astype(jnp.float32), (TILE, count))
    marks = marks.astype(jnp.bfloat16)

    smalls[2].wait()
    gains = jnp.transpose(jnp.broadcast_to(gain_ref[...], (LANES, lat)))
    gains = jnp.concatenate([gains] * (count // LANES), axis=1)
    smalls[0].wait()
    wide = latent_ref[:lat, :].astype(jnp.float32)
    factor = lax.rsqrt(jnp.mean(wide * wide, axis=0, keepdims=True) + 1e-06)
    renewed[:lat, :] = (wide * factor * gains).astype(jnp.bfloat16)
    renewed[lat:width, :] = latent_ref[lat:, :]
    renewed[width:, :] = jnp.zeros((lat + LANES - width, count), jnp.bfloat16)

    def swap(packed):
        return jnp.concatenate([packed[..., rope:], packed[..., :rope]], axis=-1)

    def fill(owner_group):
        first = owner_group * part
        choose = (
            lax.broadcasted_iota(jnp.int32, (part, count), 0) + first == target
        ).astype(jnp.float32).astype(jnp.bfloat16)
        main = lax.dot_general(choose, renewed[:lat, :], NT, preferred_element_type=jnp.float32)
        tail = lax.dot_general(choose, renewed[lat:, :], NT, preferred_element_type=jnp.float32)
        mark = lax.dot_general(marks, choose, NT, preferred_element_type=jnp.float32)
        where = pl.ds(owner_group * group, group)
        send_rows[where] = main.astype(jnp.bfloat16).reshape(group, cap, lat)
        tail = tail.reshape(group, cap, LANES)
        send_tails[where] = (tail[:, :half] + swap(tail[:, half:])).astype(jnp.bfloat16)
        for i in range(group):
            one = mark[:1, i * cap : (i + 1) * cap]
            send_marks[owner_group * group + i] = jnp.concatenate([one, one], axis=1)

    class Several:
        def __init__(self, copies):
            self.copies = copies

        def start(self):
            for copy in self.copies:
                copy.start()

        def wait(self):
            for copy in self.copies:
                copy.wait()

        def wait_send(self):
            for copy in self.copies:
                copy.wait_send()

        def wait_recv(self):
            for copy in self.copies:
                copy.wait_recv()

    pairs = [(send_marks, got_marks), (send_tails, got_tails), (send_rows, got_rows)]

    def row_copy(step):
        peer = flip(me, step)
        return Several(
            [
                pltpu.make_async_remote_copy(
                    src_ref=sent.at[peer],
                    dst_ref=got.at[step],
                    send_sem=row_send.at[i, step],
                    recv_sem=row_recv.at[i, step],
                    device_id={"ep": peer},
                    device_id_type=pl.DeviceIdType.MESH,
                )
                for i, (sent, got) in enumerate(pairs)
            ]
        )

    my_group = me // group
    for index, bits in enumerate(turns):
        fill(flip(my_group, bits))
        if index == 0:
            pl.semaphore_wait(barrier, n - 1)
        for step in range(max(bits * group, 1), (bits + 1) * group):
            row_copy(step).start()
    own_rows = Several(
        [
            pltpu.make_async_copy(sent.at[me], got.at[0], own_sem.at[1 + i])
            for i, (sent, got) in enumerate(pairs)
        ]
    )
    own_rows.start()

    smalls[3].wait()

    loads[0].wait()
    for r in range(req):
        halves, tails = [], []
        for q in range(qrows):
            turned = jnp.transpose(raw_queries[r, q].astype(jnp.float32))
            halves.append(turned[:, :lat].reshape(n, hpd, lat))
            tails.append(turned[:, lat:].reshape(n, hpd, rope))
        main = jnp.concatenate(halves, axis=1).reshape(rows_req, lat)
        tail = jnp.concatenate(tails, axis=1).reshape(rows_req, rope)
        tail = jnp.concatenate([tail, jnp.zeros((rows_req, LANES - rope), jnp.float32)], axis=1)
        queries[pl.ds(r * rows_req, rows_req), :lat] = main.astype(jnp.bfloat16)
        queries[pl.ds(r * rows_req, rows_req), lat:] = tail.astype(jnp.bfloat16)

    def absorb(where, scores, values, form, fresh):
        top = jnp.max(scores, axis=1, keepdims=True)
        if not fresh:
            was = highest[where, :1]
            top = jnp.maximum(top, was)
            keep = jnp.exp(was - top)
        weights = jnp.exp(scores - top)
        mass = jnp.sum(weights, axis=1, keepdims=True)
        blend = lax.dot_general(
            weights.astype(jnp.bfloat16), values, form, preferred_element_type=jnp.float32
        )
        if not fresh:
            mass = mass + denom[where, :1] * keep
            blend = blend + total[where, :] * keep
        highest[where, :] = jnp.broadcast_to(top, (top.shape[0], LANES))
        denom[where, :] = jnp.broadcast_to(mass, (top.shape[0], LANES))
        total[where, :] = blend

    for r in range(req):
        loads[1 + r].wait()
        where = pl.ds(r * rows_req, rows_req)
        limit = length_ref[r]

        def early(i, fresh):
            keys = old_rows[r, :, pl.ds(pl.multiple_of(i * chunk, chunk), chunk)]
            scores = scale * lax.dot_general(
                queries[where, :width], keys, NN, preferred_element_type=jnp.float32
            )
            position = i * chunk + lax.broadcasted_iota(jnp.int32, (rows_req, chunk), 1)
            scores = jnp.where(position < limit, scores, MASKED)
            absorb(where, scores, keys[:lat, :], NT, fresh)

        early(0, True)

        @pl.loop(1, old // chunk)
        def _(i):
            early(i, False)

    own_rows.wait()
    for first in range(0, n, group):
        for step in range(max(first, 1), first + group):
            row_copy(step).wait_recv()
        packed = got_tails[pl.ds(first, group)].astype(jnp.float32)
        tail = jnp.concatenate([packed, swap(packed)], axis=1).astype(jnp.bfloat16)
        values = got_rows[pl.ds(first, group)].reshape(part, lat)
        keys = jnp.concatenate([values, tail.reshape(part, LANES)], axis=1)
        low = lax.broadcasted_iota(jnp.int32, (1, LANES), 1) < cap
        mark = jnp.concatenate(
            [
                jnp.where(low, got_marks[first + i], got_marks[first + i + 1])
                for i in range(0, group, 2)
            ],
            axis=1,
        )
        for r in range(req):
            where = pl.ds(r * rows_req, rows_req)
            scores = scale * lax.dot_general(
                queries[where, :], keys, NT, preferred_element_type=jnp.float32
            )
            scores = jnp.where(mark == r + 1.0, scores, MASKED)
            absorb(where, scores, values, NN, False)

    for r in range(req):
        where = pl.ds(r * rows_req, rows_req)
        latents[r] = (
            (total[where, :] / denom[where, :1]).astype(jnp.bfloat16).reshape(n, block, lat)
        )

    def latent_copy(step):
        peer = flip(me, step)
        return pltpu.make_async_remote_copy(
            src_ref=latents.at[:, peer],
            dst_ref=got_latents.at[step],
            send_sem=lat_send.at[step],
            recv_sem=lat_recv.at[step],
            device_id={"ep": peer},
            device_id_type=pl.DeviceIdType.MESH,
        )

    for bits in turns:
        for step in range(max(bits * group, 1), (bits + 1) * group):
            latent_copy(step).start()
    own_latents = pltpu.make_async_copy(latents.at[:, me], got_latents.at[0], own_sem.at[0])
    own_latents.start()

    loads[1 + req].wait()
    for step in range(1, n):
        row_copy(step).wait_send()
    own_latents.wait()
    rows = req * block
    head_of = lax.broadcasted_iota(jnp.int32, (group * rows, out_ref.shape[1]), 0) % hpd
    for first in range(0, n, group):
        for step in range(max(first, 1), first + group):
            latent_copy(step).wait_recv()
        left = got_latents[pl.ds(first, group)].reshape(group * rows, lat)
        result = jnp.zeros(head_of.shape, jnp.float32)
        for h in range(hpd):
            value = jnp.dot(left, up[h], preferred_element_type=jnp.float32)
            result = jnp.where(head_of == h, value, result)
        result = result.astype(jnp.bfloat16)
        for i in range(group):
            source = flip(me, first + i)
            out_ref[pl.ds(source * rows, rows), :] = result[i * rows : (i + 1) * rows]
    for step in range(1, n):
        latent_copy(step).wait_send()


def fused(new_latent, latent_gain, row_slot, old_length, cache, queries, value_up):
    n = lax.axis_size("ep")
    req, cache_len, width = cache.shape
    lat = latent_gain.shape[0]
    count = new_latent.shape[0]
    cap = 2 * count // n
    qrows, heads = queries.shape[1:3]
    hpd, _, hd = value_up.shape
    scale = (hd + width - lat) ** (-0.5)
    old = cache_len // 2
    rows_req = qrows * heads
    block = qrows * hpd
    dims = (n, req, cache_len, width, lat, cap, heads, qrows, scale, min(512, old))
    bf16, f32 = jnp.bfloat16, jnp.float32
    vmem = pl.BlockSpec(memory_space=pltpu.VMEM)
    hbm = pl.BlockSpec(memory_space=pl.ANY)
    wide = lat + LANES
    out = pl.pallas_call(
        functools.partial(kernel, dims),
        out_shape=jax.ShapeDtypeStruct((n * req * block, hd), bf16),
        in_specs=[hbm] * 7,
        out_specs=vmem,
        scratch_shapes=[
            pltpu.VMEM((width, count), bf16),
            pltpu.VMEM((1, lat), f32),
            pltpu.VMEM((1, count), jnp.int32),
            pltpu.SMEM((req,), jnp.int32),
            pltpu.VMEM((wide, count), bf16),
            pltpu.VMEM((n, cap, lat), bf16),
            pltpu.VMEM((n, cap, lat), bf16),
            pltpu.VMEM((n, cap // 2, LANES), bf16),
            pltpu.VMEM((n, cap // 2, LANES), bf16),
            pltpu.VMEM((n, 1, LANES), f32),
            pltpu.VMEM((n, 1, LANES), f32),
            pltpu.VMEM((req, width, old), bf16),
            pltpu.VMEM((req * rows_req, wide), bf16),
            pltpu.VMEM((req, qrows, width, heads), bf16),
            pltpu.VMEM(value_up.shape, bf16),
            pltpu.VMEM((req * rows_req, lat), f32),
            pltpu.VMEM((req * rows_req, LANES), f32),
            pltpu.VMEM((req * rows_req, LANES), f32),
            pltpu.VMEM((req, n, block, lat), bf16),
            pltpu.VMEM((n, req, block, lat), bf16),
            pltpu.SemaphoreType.DMA((3, n)),
            pltpu.SemaphoreType.DMA((3, n)),
            pltpu.SemaphoreType.DMA((n,)),
            pltpu.SemaphoreType.DMA((n,)),
            pltpu.SemaphoreType.DMA((4,)),
            pltpu.SemaphoreType.DMA((req + 2,)),
            pltpu.SemaphoreType.DMA((4,)),
        ],
        compiler_params=pltpu.CompilerParams(
            collective_id=0, has_side_effects=True, vmem_limit_bytes=63 * 1024 * 1024
        ),
        cost_estimate=pl.CostEstimate(
            flops=2 * req * rows_req * (old + n * cap) * (width + lat),
            bytes_accessed=2 * req * old * width,
            transcendentals=req * rows_req * (old + n * cap),
        ),
    )(
        new_latent.T,
        latent_gain[None, :],
        row_slot[None, :],
        old_length,
        jnp.swapaxes(cache, 1, 2),
        jnp.swapaxes(queries, 2, 3),
        value_up,
    )
    return out.reshape(n * req, qrows, hpd, hd)


def normalize(latent_rows, gains):
    widened = latent_rows.astype(jnp.float32)
    latent_width = gains.shape[0]
    latent_part = widened[:, :latent_width]
    factor = lax.rsqrt(jnp.mean(latent_part * latent_part, axis=1, keepdims=True) + 1e-06)
    return jnp.concatenate(
        [latent_part * factor * gains[None, :], widened[:, latent_width:]], axis=1
    ).astype(jnp.bfloat16)


def masked_scores(query_rows, key_rows, usable, score_scale):
    scores = (
        lax.dot_general(
            query_rows, key_rows, (((1,), (1,)), ((), ())), preferred_element_type=jnp.float32
        )
        * score_scale
    )
    return jnp.where(usable[None, :], scores, -1e30)


def collective(new_latent, latent_gain, row_slot, old_length, cache, queries, value_up):
    device_count = lax.axis_size("ep")
    req_count, cache_len, row_width = cache.shape
    latent_width = latent_gain.shape[0]
    row_count = new_latent.shape[0]
    capacity = 2 * row_count // device_count
    local_slots = req_count * cache_len
    query_count = queries.shape[1]
    head_count = queries.shape[2]
    score_scale = (value_up.shape[2] + row_width - latent_width) ** (-0.5)
    renewed = normalize(new_latent, latent_gain)
    owners = row_slot // local_slots
    belongs = (owners[:, None] == jnp.arange(device_count, dtype=jnp.int32)[None, :]).astype(
        jnp.int32
    )
    earlier = jnp.cumsum(belongs, axis=0) - belongs
    order_rank = jnp.sum(earlier * belongs, axis=1)
    target = owners * capacity + order_rank
    send_rows = (
        jnp.zeros((device_count * capacity, row_width), jnp.bfloat16).at[target].set(renewed)
    )
    send_rows = send_rows.reshape(device_count, capacity, row_width)
    send_slots = (
        jnp.full((device_count * capacity,), -1, jnp.int32)
        .at[target]
        .set(row_slot - owners * local_slots)
    )
    send_slots = send_slots.reshape(device_count, capacity)
    positions = jnp.arange(cache_len, dtype=jnp.int32)
    got_rows, got_slots = (
        lax.all_to_all(send_rows, "ep", split_axis=0, concat_axis=0, tiled=True),
        lax.all_to_all(send_slots, "ep", split_axis=0, concat_axis=0, tiled=True),
    )
    got_rows = got_rows.reshape(device_count * capacity, row_width)
    got_slots = got_slots.reshape(device_count * capacity)
    outputs = []
    old_len = cache_len // 2
    for request in range(req_count):
        query_rows = queries[request].reshape(query_count * head_count, row_width)
        old_rows = cache[request, :old_len]
        early_scores = masked_scores(
            query_rows, old_rows, positions[:old_len] < old_length[request], score_scale
        )
        owned = (got_slots >= 0) & (got_slots // cache_len == request)
        late_scores = masked_scores(query_rows, got_rows, owned, score_scale)
        highest = jnp.maximum(
            jnp.max(early_scores, axis=1, keepdims=True),
            jnp.max(late_scores, axis=1, keepdims=True),
        )
        early_weights = jnp.exp(early_scores - highest)
        late_weights = jnp.exp(late_scores - highest)
        denominator = jnp.sum(early_weights, axis=1, keepdims=True) + jnp.sum(
            late_weights, axis=1, keepdims=True
        )
        blended = jnp.dot(
            early_weights.astype(jnp.bfloat16), old_rows, preferred_element_type=jnp.float32
        )
        blended = blended + jnp.dot(
            late_weights.astype(jnp.bfloat16), got_rows, preferred_element_type=jnp.float32
        )
        blended = blended[:, :latent_width] / denominator
        outputs.append(blended.astype(jnp.bfloat16).reshape(query_count, head_count, latent_width))
    latent_out = jnp.stack(outputs, axis=0)
    return jnp.einsum(
        "rqhl,hld->rqhd",
        lax.all_to_all(latent_out, "ep", split_axis=2, concat_axis=0, tiled=True),
        value_up,
        preferred_element_type=jnp.float32,
    ).astype(jnp.bfloat16)


def local(*args):
    new_latent, latent_gain, _, _, cache, queries, value_up = args
    n = lax.axis_size("ep")
    lat = latent_gain.shape[0]
    rope = cache.shape[2] - lat
    whole_tiles = (
        n % 4 == 0
        and n & (n - 1) == 0
        and 4 * new_latent.shape[0] // n == LANES
        and (queries.shape[1] * value_up.shape[0]) % TILE == 0
        and value_up.shape[0] % 8 == 0
        and lat % LANES == 0
        and new_latent.shape[0] % LANES == 0
        and queries.shape[2] % LANES == 0
        and 2 * rope == LANES
    )
    return fused(*args) if whole_tiles else collective(*args)


def solution(mesh):
    in_specs = (
        P(("groups", "ep"), None),
        P(),
        P(("groups", "ep")),
        P(("groups", "ep")),
        P(("groups", "ep"), None, None),
        P(("groups", "ep"), None, None, None),
        P("ep", None, None),
    )
    out_specs = P("groups", None, "ep", None)
    return jax.shard_map(local, mesh=mesh, in_specs=in_specs, out_specs=out_specs, check_vma=False)
```
